32 devices in a mesh: dp: 8 (over y, x, core), tensor: 4 (over z).
Axes of the slice: x: 2, y: 2, z: 4, core: 2. Of those that a mesh axis runs over, the one named last changes fastest.
Arguments:
- inputs: bfloat16 [8192, 1024], P('dp'), may hold values from -6 to 6
- cotangent: bfloat16 [8192, 1024], P('dp'), may hold values from -6 to 6
- lengths: int32 [8, 8], P('dp'), may hold values from 1 to 256, 1024 in all within a row
- ln1_gain: float32 [1024], replicated, may hold values from 0.5 to 1.5
- ln1_bias: float32 [1024], replicated, may hold values from -3 to 3
- w_query: bfloat16 [1024, 1024], replicated, may hold values from -0.1875 to 0.1875
- w_key: bfloat16 [1024, 1024], replicated, may hold values from -0.1875 to 0.1875
- w_value: bfloat16 [1024, 1024], replicated, may hold values from -0.1875 to 0.1875
- w_out: bfloat16 [1024, 1024], replicated, may hold values from -0.75 to 0.75
- ln2_gain: float32 [1024], replicated, may hold values from 0.5 to 1.5
- ln2_bias: float32 [1024], replicated, may hold values from -3 to 3
- w_up: bfloat16 [1024, 4096], P(None, 'tensor'), may hold values from -0.1875 to 0.1875
- b_up: float32 [4096], P('tensor'), may hold values from -4 to 4
- w_down: bfloat16 [4096, 1024], P('tensor'), may hold values from -0.09375 to 0.09375
- b_down: float32 [1024], replicated, may hold values from -4 to 4
Outputs:
- output: bfloat16 [8192, 1024], P('dp')
- grad_input: float32 [8192, 1024], P('dp')
- grad_ln1_gain: float32 [1024], P('dp')
- grad_ln1_bias: float32 [1024], P('dp')
- grad_w_query: float32 [1024, 1024], P('dp')
- grad_w_key: float32 [1024, 1024], P('dp')
- grad_w_value: float32 [1024, 1024], P('dp')
- grad_w_out: float32 [1024, 1024], P('dp')
- grad_ln2_gain: float32 [1024], P('dp')
- grad_ln2_bias: float32 [1024], P('dp')
- grad_w_up: float32 [1024, 4096], P('dp', 'tensor')
- grad_b_up: float32 [4096], P(('tensor', 'dp'))
- grad_w_down: float32 [4096, 1024], P('tensor', 'dp')
- grad_b_down: float32 [1024], P('dp')
The draws below stay inside these ranges and needn't reach their ends.
Inputs may be any that keep to these rules, and one draw needn't show every extreme that they name: Each row's 8 lengths sum to 1024, and the largest of each row is 256.
All inputs are finite; a program needn't handle non-finite values.
Results may differ from the reference program's by a relative error of at most 0.012.
Values may be sent and summed in bfloat16 or wider, within the bound.
A program may use at most 192 MiB of HBM per device.

```python
import math
import jax
import jax.numpy as jnp
import numpy as np
from jax import lax

D = 1024
HEADS = 16
HEAD_DIM = 64
FF = 4096
ROW_LEN = 1024
NIMG = 8
IMG_MOST = 256
ROWS = 8
TOKENS = 8192


def steps_of(stream_key, shape, shards, low, high):
    level = 1.0
    for axis_at, blocks in shards:
        draws = jax.random.uniform(jax.random.fold_in(jax.random.fold_in(stream_key, 6), axis_at), (blocks,), jnp.float32, low / len(shards), high / len(shards))
        level = level * jnp.repeat(jnp.exp(draws), shape[axis_at] // blocks).reshape((-1,) + (1,) * (len(shape) - 1 - axis_at))
    return level


def split_up(number_of, total, bound, skew):
    weights = [(1 << 20) // math.isqrt(grade ** skew) + 1 for grade in range(2, number_of + 1)]
    spare, given = total - bound - (number_of - 1), [1] * (number_of - 1)
    while spare > 0:
        candidates = [i for i in range(number_of - 1) if given[i] < bound]
        whole, left = sum([weights[i] for i in candidates]), spare
        for i in candidates:
            addition = min(bound - given[i], max(1, left * weights[i] // whole), spare)
            given[i] = given[i] + addition
            spare = spare - addition
    return np.array([bound] + given)


def uneven_parts(rng, count, total, most, skew):
    if count == 2:
        one = jax.random.randint(rng, (), max(1, total - most), min(most, total - 1) + 1)
        return jnp.stack([one, total - one])
    sizes = jnp.asarray(split_up(count, total, most, skew), jnp.int32)
    twos = (count - 1) // 2
    source_of, taker = sizes[1:1 + 2 * twos:2], sizes[2:2 + 2 * twos:2]
    margin = jnp.minimum(source_of - 1, most - taker)
    shifted = jax.random.randint(jax.random.fold_in(rng, 1), (twos,), 0, 1 << 20) % (margin + 1)
    sizes = sizes.at[1:1 + 2 * twos:2].set(source_of - shifted).at[2:2 + 2 * twos:2].set(taker + shifted)
    return sizes[jax.random.permutation(jax.random.fold_in(rng, 2), count)]


def gaussian(stream_key, extent, scale, bound, shards=(), kind=jnp.bfloat16):
    loudness = steps_of(stream_key, extent, shards, -0.22, 0.18) if shards else 1.0
    drawn = jax.random.normal(stream_key, extent, jnp.float32) * scale * loudness
    return jnp.minimum(jnp.maximum(drawn, -bound), bound).astype(kind)


def setup_inputs(seed: int = 0) -> dict:
    streams_of = jax.random.split(jax.random.key(seed), 16)
    inputs = gaussian(streams_of[0], (TOKENS, D), 1.0, 6.0, ((0, 8),))
    cotangent = gaussian(streams_of[1], (TOKENS, D), 1.0, 6.0, ((0, 8),))
    lengths = jax.vmap(lambda own: uneven_parts(own, NIMG, ROW_LEN, IMG_MOST, 2))(jax.random.split(streams_of[2], ROWS)).reshape((ROWS, NIMG)).astype(jnp.int32)
    ln1_gain = jnp.clip(1.0 + 0.1 * jax.random.normal(streams_of[3], (D,), jnp.float32), 0.5, 1.5)
    ln1_bias = gaussian(streams_of[4], (D,), 0.2, 3.0, (), jnp.float32)
    w_query = gaussian(streams_of[5], (D, D), D ** -0.5, 0.1875)
    w_key = gaussian(streams_of[6], (D, D), D ** -0.5, 0.1875)
    w_value = gaussian(streams_of[7], (D, D), D ** -0.5, 0.1875)
    w_out = gaussian(streams_of[8], (D, D), (D // 16) ** -0.5, 0.75)
    ln2_gain = jnp.clip(1.0 + 0.1 * jax.random.normal(streams_of[9], (D,), jnp.float32), 0.5, 1.5)
    ln2_bias = gaussian(streams_of[10], (D,), 0.2, 3.0, (), jnp.float32)
    w_up = gaussian(streams_of[11], (D, FF), D ** -0.5, 0.1875, ((1, 4),))
    b_up = gaussian(streams_of[12], (FF,), 0.3, 4.0, ((0, 4),), jnp.float32)
    w_down = gaussian(streams_of[13], (FF, D), FF ** -0.5, 0.09375, ((0, 4),))
    b_down = gaussian(streams_of[14], (D,), 0.3, 4.0, (), jnp.float32)
    return dict(inputs=inputs, cotangent=cotangent, lengths=lengths, ln1_gain=ln1_gain, ln1_bias=ln1_bias, w_query=w_query, w_key=w_key, w_value=w_value, w_out=w_out, ln2_gain=ln2_gain, ln2_bias=ln2_bias, w_up=w_up, b_up=b_up, w_down=w_down, b_down=b_down)


@jax.custom_vjp
def low(v):
    return lax.optimization_barrier(v.astype(jnp.bfloat16)).astype(jnp.float32)

@jax.custom_vjp
def low_back(v):
    return v

def low_keep(v):
    return (low(v), None)

def low_pass(kept, grad):
    return (grad,)

def back_keep(v):
    return (v, None)

def back_low(kept, grad):
    return (low(grad),)
low.defvjp(low_keep, low_pass)
low_back.defvjp(back_keep, back_low)

def layer_norm(values, gain, shift):
    average = lax.optimization_barrier(jnp.mean(values, axis=-1, keepdims=True))
    centered = values - average
    variance = lax.optimization_barrier(jnp.mean(centered * centered, axis=-1, keepdims=True))
    return centered * lax.rsqrt(variance + 1e-05) * gain + shift

def matmul(left, right):
    return jnp.dot(left, right, precision=lax.Precision.HIGHEST, preferred_element_type=jnp.float32)

def row_attention(packed):
    queries, keys, values, segment = packed
    length = queries.shape[0]
    feat_query = (jax.nn.elu(queries) + 1.0).reshape(length, HEADS, HEAD_DIM)
    feat_key = (jax.nn.elu(keys) + 1.0).reshape(length, HEADS, HEAD_DIM)
    feat_value = values.reshape(length, HEADS, HEAD_DIM)
    places = jnp.arange(length, dtype=jnp.int32)
    allowed = (places[:, None] >= places[None, :]) & (segment[:, None] == segment[None, :])
    scores = jnp.einsum('thd,shd->hts', feat_query, feat_key, precision=lax.Precision.HIGHEST)
    scores = jnp.where(allowed[None], scores, 0.0)
    numer = jnp.einsum('hts,she->the', scores, feat_value, precision=lax.Precision.HIGHEST)
    denom = lax.optimization_barrier(jnp.sum(scores, axis=-1)).T
    return (numer / denom[:, :, None]).reshape(length, HEADS * HEAD_DIM)

def reference(inputs, cotangent, lengths, ln1_gain, ln1_bias, w_query, w_key, w_value, w_out, ln2_gain, ln2_bias, w_up, b_up, w_down, b_down):
    image_ends = jnp.cumsum(lengths, axis=1).astype(jnp.int32)
    places = jnp.arange(ROW_LEN, dtype=jnp.int32)
    segments = lax.optimization_barrier(jnp.sum((places[None, :, None] >= image_ends[:, None, :]).astype(jnp.int32), axis=-1))

    def forward(residual, gain_one, bias_one, weight_query, weight_key, weight_value, weight_out, gain_two, bias_two, weight_up, bias_up, weight_down, bias_down):
        normed_one = low(layer_norm(residual, gain_one, bias_one))
        queries = low_back(low(matmul(normed_one, weight_query)))
        keys = low_back(low(matmul(normed_one, weight_key)))
        values = low_back(low(matmul(normed_one, weight_value)))
        attended = lax.map(jax.checkpoint(row_attention), (queries.reshape(-1, ROW_LEN, D), keys.reshape(-1, ROW_LEN, D), values.reshape(-1, ROW_LEN, D), segments))
        attended = low(attended.reshape(-1, D))
        middle = residual + low_back(matmul(attended, weight_out))
        normed_two = low(layer_norm(middle, gain_two, bias_two))
        up_proj = low_back(matmul(normed_two, weight_up) + bias_up)
        hidden = low(jax.nn.gelu(up_proj))
        down = low_back(matmul(hidden, weight_down))
        return middle + down + bias_down
    floats = (inputs.astype(jnp.float32), ln1_gain, ln1_bias, w_query.astype(jnp.float32), w_key.astype(jnp.float32), w_value.astype(jnp.float32), w_out.astype(jnp.float32), ln2_gain, ln2_bias, w_up.astype(jnp.float32), b_up, w_down.astype(jnp.float32), b_down)
    result, backward = jax.vjp(forward, *floats)
    grads = backward(cotangent.astype(jnp.float32))
    return (result.astype(jnp.bfloat16), grads[0], grads[1], grads[2], grads[3], grads[4], grads[5], grads[6], grads[7], grads[8], grads[9], grads[10], grads[11], grads[12])
```

```python
import functools

import jax
import jax.numpy as jnp
from jax import lax
from jax.experimental import pallas as pl
from jax.experimental.pallas import tpu as pltpu
from jax.sharding import PartitionSpec as P

EPS = 1e-05
BLK = 256
PAIR = 128
HEAD = 64
C0 = 0.7978845608028654
C1 = 0.044715
F32 = jnp.float32
BF = jnp.bfloat16
VM = pltpu.VMEM


def nn(a, b):
    return lax.dot_general(a, b, (((1,), (0,)), ((), ())), preferred_element_type=F32)


def nt(a, b):
    return lax.dot_general(a, b, (((1,), (1,)), ((), ())), preferred_element_type=F32)


def tn(a, b):
    return lax.dot_general(a, b, (((0,), (0,)), ((), ())), preferred_element_type=F32)


def mean(v):
    return jnp.mean(v, axis=-1, keepdims=True)


def normed(v):
    centered = v - mean(v)
    scale = lax.rsqrt(mean(centered * centered) + EPS)
    return centered * scale, scale


def norm_back(e, hat, scale, gain):
    eg = e * gain
    return scale * (eg - mean(eg) - hat * mean(eg * hat))


def feature(v):
    return jnp.where(v > 0, v + 1.0, jnp.exp(jnp.minimum(v, 0.0)))


def ends_of(len_ref, n_images):
    ends, total = [], 0
    for i in range(n_images):
        total = total + len_ref[0, i]
        ends.append(total)
    return ends


def segment_of(places, ends):
    seg = jnp.zeros(places.shape, jnp.int32)
    for end in ends:
        seg = seg + jnp.where(places >= end, 1, 0)
    return seg


def scalar_segment(place, ends):
    seg = 0
    for end in ends:
        seg = seg + jnp.where(place >= end, 1, 0)
    return seg


def head_masks():
    lane = lax.broadcasted_iota(jnp.int32, (1, PAIR), 1)
    first = jnp.where(lane < HEAD, 1.0, 0.0).astype(BF)
    return first, (1.0 - first.astype(F32)).astype(BF)


def block_diagonal():
    row = lax.broadcasted_iota(jnp.int32, (PAIR, 2 * PAIR), 0)
    lane = lax.broadcasted_iota(jnp.int32, (PAIR, 2 * PAIR), 1)
    return jnp.where((row < HEAD) == (lax.rem(lane, PAIR) < HEAD), 1.0, 0.0)


def block_masks(b, ends):
    col = segment_of(b * BLK + lax.broadcasted_iota(jnp.int32, (BLK, 1), 0), ends)
    row = segment_of(b * BLK + lax.broadcasted_iota(jnp.int32, (1, BLK), 1), ends)
    before = jnp.where(b > 0, scalar_segment(b * BLK - 1, ends), -1)
    last = scalar_segment(b * BLK + BLK - 1, ends)
    t = lax.broadcasted_iota(jnp.int32, (BLK, BLK), 0)
    s = lax.broadcasted_iota(jnp.int32, (BLK, BLK), 1)
    same = col == row
    down = jnp.where(same & (t >= s), 1.0, 0.0).astype(BF)
    up = jnp.where(same & (t <= s), 1.0, 0.0).astype(BF)
    cont = jnp.where(col == before, 1.0, 0.0).astype(BF)
    trail = jnp.where(col == last, 1.0, 0.0).astype(BF)
    return down, up, cont, trail


def two(v):
    return jnp.concatenate([v, v], axis=0)


def forward_kernel(
    n_images,
    len_ref, g1, b1, g2, b2, bup,
    x_h, cot_h, wq_h, wk_h, wv_h, wo_h, wu_h, wd_h,
    n1_h, pq_h, pk_h, va_h, rd_h, at_h, al_h, st_h, mid_h, pn_h, pd_h, gwu_h, gwd_h, vec_ref,
    x, cot, wq, wk, wv, wo, wu, wd,
    n1, pq, pk, va, rd, at, al, st, mid, n2, hid, gu, pn, pd, gw,
    in_sem, out_sem,
):
    rows_all = x.shape[0]
    blocks = rows_all // BLK
    width = x.shape[1]
    loads = [(x_h, x), (wq_h, wq), (wk_h, wk), (wv_h, wv), (wo_h, wo), (wu_h, wu), (cot_h, cot), (wd_h, wd)]
    loads = [pltpu.make_async_copy(s, d, in_sem.at[i]) for i, (s, d) in enumerate(loads)]
    for c in loads:
        c.start()
    ends = ends_of(len_ref, n_images)
    m0, m1 = head_masks()
    ones = jnp.ones((BLK, PAIR), BF)
    diagonal = block_diagonal()
    vec_ref[...] = jnp.zeros_like(vec_ref)
    for c in loads:
        c.wait()

    saved = [(n1, n1_h), (pq, pq_h), (pk, pk_h), (va, va_h), (rd, rd_h), (at, at_h), (al, al_h), (mid, mid_h), (pn, pn_h), (pd, pd_h)]

    def one_block(b, _):
        rows = pl.ds(pl.multiple_of(b * BLK, BLK), BLK)
        xb = x[rows, :].astype(F32)
        hat, _ = normed(xb)
        n1b = (hat * g1[...] + b1[...]).astype(BF)
        n1[rows, :] = n1b
        pq[rows, :] = feature(nn(n1b, wq[...]).astype(BF).astype(F32)).astype(BF)
        pk[rows, :] = feature(nn(n1b, wk[...]).astype(BF).astype(F32)).astype(BF)
        va[rows, :] = nn(n1b, wv[...]).astype(BF)
        down, _, cont, trail = block_masks(b, ends)
        down2 = two(down)
        for p in range(width // PAIR):
            lanes = slice(p * PAIR, (p + 1) * PAIR)
            q, k, v = pq[rows, lanes], pk[rows, lanes], va[rows, lanes]
            a = nt(jnp.concatenate([q * m0, q * m1], axis=0), k).astype(BF) * down2
            o = nn(a[:BLK], jnp.concatenate([v * m0, ones * m0], axis=1))
            o = o + nn(a[BLK:], jnp.concatenate([v * m1, ones * m1], axis=1))
            before = jnp.where(b > 0, st[jnp.maximum(b - 1, 0), p].astype(F32), 0.0).astype(BF)
            o = o + nn(q * cont, before)
            st[b, p] = (tn(k * trail, jnp.concatenate([v, ones], axis=1)) * diagonal).astype(BF)
            inverse = 1.0 / o[:, PAIR:]
            rd[rows, lanes] = inverse.astype(BF)
            attended = o[:, :PAIR] * inverse
            attended_low = attended.astype(BF)
            at[rows, lanes] = attended_low
            al[rows, lanes] = (attended - attended_low.astype(F32)).astype(BF)
        middle = xb + nn(at[rows, :], wo[...])
        mid[rows, :] = middle
        hat2, _ = normed(middle)
        n2b = (hat2 * g2[...] + b2[...]).astype(BF)
        n2[rows, :] = n2b
        cb = cot[rows, :]
        vec_ref[0:1, :] += jnp.sum(cb.astype(F32), axis=0, keepdims=True)
        for c in range(width // BLK):
            cols = slice(c * BLK, (c + 1) * BLK)
            u = nn(n2b, wu[:, cols]) + bup[:, cols]
            gh = nt(cb, wd[cols, :])
            th = jnp.tanh(C0 * (u + C1 * u * u * u))
            hid[rows, cols] = (0.5 * u * (1.0 + th)).astype(BF)
            slope = 0.5 * (1.0 + th) + 0.5 * u * (1.0 - th * th) * (C0 * (1.0 + 3.0 * C1 * u * u))
            gub = (gh * slope).astype(BF)
            gu[rows, cols] = gub
            vec_ref[1:2, cols] += jnp.sum(gub.astype(F32), axis=0, keepdims=True)
        pn[rows, :] = nt(gu[rows, :], wu[...]).astype(BF)
        pd[rows, :] = nn(hid[rows, :], wd[...]).astype(BF)
        for i, (s, d) in enumerate(saved):
            pltpu.make_async_copy(s.at[rows, :], d.at[rows, :], out_sem.at[i, b]).start()
        return 0

    lax.fori_loop(0, blocks, one_block, 0)
    tail = pltpu.make_async_copy(st, st_h, out_sem.at[len(saved), 0])
    tail.start()
    for g, (l, r, d) in enumerate(((n2, gu, gwu_h), (hid, cot, gwd_h))):
        for c in range(width // BLK):
            cols = slice(c * BLK, (c + 1) * BLK)
            gw[g, :, cols] = tn(l[...], r[:, cols]).astype(BF)
        pltpu.make_async_copy(gw.at[g], d, out_sem.at[len(saved), 1 + g]).start()
    tail.wait()
    for g, d in enumerate((gwu_h, gwd_h)):
        pltpu.make_async_copy(gw.at[g], d, out_sem.at[len(saved), 1 + g]).wait()
    for b in range(blocks):
        rows = pl.ds(b * BLK, BLK)
        for i, (s, d) in enumerate(saved):
            pltpu.make_async_copy(s.at[rows, :], d.at[rows, :], out_sem.at[i, b]).wait()


def backward_kernel(
    n_images,
    len_ref, g1, g2, bd,
    x_h, cot_h, wq_h, wk_h, wv_h, wo_h, n1_h, pq_h, pk_h, va_h, rd_h, at_h, al_h, st_h, mid_h, tot_h, down_h,
    out_h, gi_h, gq_h, gk_h, gv_h, go_h, vec_ref,
    x, cot, wq, wk, wv, wo, n1, pq, pk, va, rd, at, al, st, mid, tot, down,
    gb, nv, mm, gq, gk, gv, gw, carry,
    in_sem, out_sem,
):
    rows_all = x.shape[0]
    blocks = rows_all // BLK
    width = x.shape[1]
    loads = [(mid_h, mid), (tot_h, tot), (cot_h, cot), (wo_h, wo), (at_h, at), (al_h, al), (rd_h, rd), (pq_h, pq), (pk_h, pk), (va_h, va),
             (st_h, st), (wq_h, wq), (wk_h, wk), (wv_h, wv), (x_h, x), (n1_h, n1), (down_h, down)]
    loads = [pltpu.make_async_copy(s, d, in_sem.at[i]) for i, (s, d) in enumerate(loads)]
    for c in loads:
        c.start()
    ends = ends_of(len_ref, n_images)
    m0, m1 = head_masks()
    ones = jnp.ones((BLK, PAIR), BF)
    diagonal = block_diagonal()
    row = lax.broadcasted_iota(jnp.int32, (2 * PAIR, 2 * PAIR), 0) // HEAD
    lane = lax.broadcasted_iota(jnp.int32, (2 * PAIR, 2 * PAIR), 1) // HEAD
    same_head = jnp.where(row == lane, 1.0, 0.0).astype(BF)
    half = lax.rem(lax.broadcasted_iota(jnp.int32, (1, BLK), 1), HEAD) < HEAD // 2
    vec_ref[...] = jnp.zeros_like(vec_ref)
    carry[...] = jnp.zeros_like(carry)
    for c in loads:
        c.wait()

    def norm_block(b, _):
        rows = pl.ds(pl.multiple_of(b * BLK, BLK), BLK)
        middle = mid[rows, :]
        hat, scale = normed(middle)
        e = tot[rows, :].astype(F32)
        vec_ref[0:1, :] += jnp.sum(e * hat, axis=0, keepdims=True)
        vec_ref[1:2, :] += jnp.sum(e, axis=0, keepdims=True)
        gm = cot[rows, :].astype(F32) + norm_back(e, hat, scale, g2[...])
        out = (middle + down[rows, :].astype(F32) + bd[...]).astype(BF)
        down[rows, :] = out
        mid[rows, :] = gm
        gbb = gm.astype(BF)
        gb[rows, :] = gbb
        ga = nt(gbb, wo[...])
        inverse = rd[rows, :].astype(F32)
        n = (ga * inverse).astype(BF)
        nv[rows, :] = n
        prod = n.astype(F32) * (at[rows, :].astype(F32) + al[rows, :].astype(F32))
        high = prod.astype(BF)
        rest = (prod - high.astype(F32)).astype(BF)
        for c in range(width // BLK):
            cols = slice(c * BLK, (c + 1) * BLK)
            m = (nn(high[:, cols], same_head) + nn(rest[:, cols], same_head)) * (-2.0 / HEAD)
            m_high = m.astype(BF).astype(F32)
            mm[rows, cols] = jnp.where(half, m_high, m - m_high).astype(BF)
        return 0

    lax.fori_loop(0, blocks, norm_block, 0)
    pltpu.make_async_copy(down, out_h, out_sem.at[0]).start()

    def core_block(i, _):
        b = blocks - 1 - i
        rows = pl.ds(pl.multiple_of(b * BLK, BLK), BLK)
        low, up, cont, trail = block_masks(b, ends)
        low2, up2 = two(low), two(up)
        for p in range(width // PAIR):
            lanes = slice(p * PAIR, (p + 1) * PAIR)
            q, k, v = pq[rows, lanes], pk[rows, lanes], va[rows, lanes]
            n, m = nv[rows, lanes], mm[rows, lanes]
            q0, q1, k0, k1, n0, n1_ = q * m0, q * m1, k * m0, k * m1, n * m0, n * m1
            nm = jnp.concatenate([n, m], axis=1)
            nm2 = jnp.concatenate(
                [jnp.concatenate([n0, m * m0], axis=1), jnp.concatenate([n1_, m * m1], axis=1)], axis=0
            )
            v1 = jnp.concatenate([v, ones], axis=1)
            v2 = jnp.concatenate(
                [jnp.concatenate([v * m0, ones * m0], axis=1), jnp.concatenate([v * m1, ones * m1], axis=1)], axis=0
            )
            da = nt(nm2, v1).astype(BF) * low2
            dat = nt(v2, nm).astype(BF) * up2
            a_t = nt(jnp.concatenate([k0, k1], axis=0), q).astype(BF) * up2
            before = jnp.where(b > 0, st[jnp.maximum(b - 1, 0), p].astype(F32), 0.0).astype(BF)
            dq = nn(da[:BLK], k0) + nn(da[BLK:], k1) + nt(nm * cont, before)
            after = carry[p]
            dk = nn(dat[:BLK], q0) + nn(dat[BLK:], q1) + nt(v1 * trail, after)
            dv = nn(a_t[:BLK], n0) + nn(a_t[BLK:], n1_) + nn(k * trail, after[:, :PAIR])
            carry[p] = (tn(q * cont, nm) * diagonal).astype(BF)
            gq[rows, lanes] = (dq * jnp.minimum(q.astype(F32), 1.0)).astype(BF)
            gk[rows, lanes] = (dk * jnp.minimum(k.astype(F32), 1.0)).astype(BF)
            gv[rows, lanes] = dv.astype(BF)
        e = nt(gq[rows, :], wq[...]) + nt(gk[rows, :], wk[...]) + nt(gv[rows, :], wv[...])
        hat, scale = normed(x[rows, :].astype(F32))
        vec_ref[2:3, :] += jnp.sum(e * hat, axis=0, keepdims=True)
        vec_ref[3:4, :] += jnp.sum(e, axis=0, keepdims=True)
        mid[rows, :] = mid[rows, :] + norm_back(e, hat, scale, g1[...])
        return 0

    lax.fori_loop(0, blocks, core_block, 0)
    pltpu.make_async_copy(mid, gi_h, out_sem.at[1]).start()
    grads = ((n1, gq, gq_h), (n1, gk, gk_h), (n1, gv, gv_h), (at, gb, go_h))
    for g, (l, r, d) in enumerate(grads):
        for c in range(width // BLK):
            cols = slice(c * BLK, (c + 1) * BLK)
            gw[g, :, cols] = tn(l[...], r[:, cols]).astype(BF)
        pltpu.make_async_copy(gw.at[g], d, out_sem.at[2 + g]).start()
    pltpu.make_async_copy(down, out_h, out_sem.at[0]).wait()
    pltpu.make_async_copy(mid, gi_h, out_sem.at[1]).wait()
    for g, (l, r, d) in enumerate(grads):
        pltpu.make_async_copy(gw.at[g], d, out_sem.at[2 + g]).wait()


def per_device(inputs, cotangent, lengths, ln1_gain, ln1_bias, w_query, w_key, w_value, w_out, ln2_gain, ln2_bias, w_up, b_up,
               w_down, b_down):
    tokens, width = inputs.shape
    n_images = lengths.shape[1]
    blocks, pairs = tokens // BLK, width // PAIR
    shape = jax.ShapeDtypeStruct
    full = shape((tokens, width), BF)
    square = shape((width, width), BF)
    anyspace = pl.BlockSpec(memory_space=pl.ANY)
    vmem = pl.BlockSpec(memory_space=VM)
    smem = pl.BlockSpec(memory_space=pltpu.SMEM)
    row = lambda v: v.reshape(1, -1)
    big = lambda dtype=BF: VM((tokens, width), dtype)
    weight = VM((width, width), BF)
    states = shape((blocks, pairs, PAIR, 2 * PAIR), BF)
    params = pltpu.CompilerParams(vmem_limit_bytes=62 << 20)
    n1, pq, pk, va, rd, at, al, st, mid, pn, pd, gwu, gwd, vec1 = pl.pallas_call(
        functools.partial(forward_kernel, n_images),
        out_shape=[full] * 7 + [states, shape((tokens, width), F32), full, full, square, square, shape((8, width), F32)],
        in_specs=[smem] + [vmem] * 5 + [anyspace] * 8,
        out_specs=[anyspace] * 13 + [vmem],
        scratch_shapes=[big(), big()] + [weight] * 6 + [big()] * 7
        + [VM((blocks, pairs, PAIR, 2 * PAIR), BF), big(F32)] + [big()] * 5 + [VM((2, width, width), BF)]
        + [pltpu.SemaphoreType.DMA((8,)), pltpu.SemaphoreType.DMA((11, blocks))],
        compiler_params=params,
    )(lengths, row(ln1_gain), row(ln1_bias), row(ln2_gain), row(ln2_bias), row(b_up),
      inputs, cotangent, w_query, w_key, w_value, w_out, w_up, w_down)
    tot = lax.psum(pn, "tensor")
    down = lax.psum(pd, "tensor")
    out, gi, gq, gk, gv, go, vec2 = pl.pallas_call(
        functools.partial(backward_kernel, n_images),
        out_shape=[full, shape((tokens, width), F32)] + [square] * 4 + [shape((8, width), F32)],
        in_specs=[smem] + [vmem] * 3 + [anyspace] * 17,
        out_specs=[anyspace] * 6 + [vmem],
        scratch_shapes=[big(), big()] + [weight] * 4 + [big()] * 7
        + [VM((blocks, pairs, PAIR, 2 * PAIR), BF), big(F32), big(), big()] + [big()] * 6 + [VM((4, width, width), BF)]
        + [VM((pairs, PAIR, 2 * PAIR), BF)]
        + [pltpu.SemaphoreType.DMA((17,)), pltpu.SemaphoreType.DMA((6,))],
        compiler_params=params,
    )(lengths, row(ln1_gain), row(ln2_gain), row(b_down),
      inputs, cotangent, w_query, w_key, w_value, w_out, n1, pq, pk, va, rd, at, al, st, mid, tot, down)
    scatter = lambda v, d=0: lax.psum_scatter(v, "dp", scatter_dimension=d, tiled=True)
    wide = lambda v: v.astype(F32)
    vec = scatter(jnp.concatenate([vec1[:2], vec2[:4]], axis=0), 1)
    return (out, gi, vec[4], vec[5], wide(scatter(gq)), wide(scatter(gk)), wide(scatter(gv)), wide(scatter(go)), vec[2], vec[3],
            wide(scatter(gwu)), vec[1], wide(scatter(gwd, 1)), vec[0])


def solution(mesh):
    rows, whole = P("dp", None), P()
    placed = (rows, rows, rows) + (whole,) * 8 + (P(None, "tensor"), P("tensor"), P("tensor", None), whole)
    return jax.shard_map(
        per_device,
        mesh=mesh,
        in_specs=placed,
        out_specs=(rows, rows, P("dp"), P("dp"), rows, rows, rows, rows, P("dp"), P("dp"), P("dp", "tensor"),
                   P(("tensor", "dp")), P("tensor", "dp"), P("dp")),
        check_vma=False,
    )
```

```python
import functools

import jax
import jax.numpy as jnp
from jax import lax
from jax.experimental import pallas as pl
from jax.experimental.pallas import tpu as pltpu
from jax.sharding import PartitionSpec as P

EPS = 1e-05
BLK = 256
PAIR = 128
HEAD = 64
C0 = 0.7978845608028654
C1 = 0.044715
F32 = jnp.float32
BF = jnp.bfloat16
VM = pltpu.VMEM


def nn(a, b):
    return lax.dot_general(a, b, (((1,), (0,)), ((), ())), preferred_element_type=F32)


def nt(a, b):
    return lax.dot_general(a, b, (((1,), (1,)), ((), ())), preferred_element_type=F32)


def tn(a, b):
    return lax.dot_general(a, b, (((0,), (0,)), ((), ())), preferred_element_type=F32)


def mean(v):
    return jnp.mean(v, axis=-1, keepdims=True)


def normed(v):
    centered = v - mean(v)
    scale = lax.rsqrt(mean(centered * centered) + EPS)
    return centered * scale, scale


def norm_back(e, hat, scale, gain):
    eg = e * gain
    return scale * (eg - mean(eg) - hat * mean(eg * hat))


def feature(v):
    return jnp.where(v > 0, v + 1.0, jnp.exp(jnp.minimum(v, 0.0)))


def ends_of(len_ref, n_images):
    ends, total = [], 0
    for i in range(n_images):
        total = total + len_ref[0, i]
        ends.append(total)
    return ends


def segment_of(places, ends):
    seg = jnp.zeros(places.shape, jnp.int32)
    for end in ends:
        seg = seg + jnp.where(places >= end, 1, 0)
    return seg


def scalar_segment(place, ends):
    seg = 0
    for end in ends:
        seg = seg + jnp.where(place >= end, 1, 0)
    return seg


def head_masks():
    lane = lax.broadcasted_iota(jnp.int32, (1, PAIR), 1)
    first = jnp.where(lane < HEAD, 1.0, 0.0).astype(BF)
    return first, (1.0 - first.astype(F32)).astype(BF)


def block_diagonal():
    row = lax.broadcasted_iota(jnp.int32, (PAIR, 2 * PAIR), 0)
    lane = lax.broadcasted_iota(jnp.int32, (PAIR, 2 * PAIR), 1)
    return jnp.where((row < HEAD) == (lax.rem(lane, PAIR) < HEAD), 1.0, 0.0)


def block_masks(b, ends):
    col = segment_of(b * BLK + lax.broadcasted_iota(jnp.int32, (BLK, 1), 0), ends)
    row = segment_of(b * BLK + lax.broadcasted_iota(jnp.int32, (1, BLK), 1), ends)
    before = jnp.where(b > 0, scalar_segment(b * BLK - 1, ends), -1)
    last = scalar_segment(b * BLK + BLK - 1, ends)
    t = lax.broadcasted_iota(jnp.int32, (BLK, BLK), 0)
    s = lax.broadcasted_iota(jnp.int32, (BLK, BLK), 1)
    same = col == row
    down = jnp.where(same & (t >= s), 1.0, 0.0).astype(BF)
    up = jnp.where(same & (t <= s), 1.0, 0.0).astype(BF)
    cont = jnp.where(col == before, 1.0, 0.0).astype(BF)
    trail = jnp.where(col == last, 1.0, 0.0).astype(BF)
    return down, up, cont, trail


def two(v):
    return jnp.concatenate([v, v], axis=0)


AR_ROWS = 128
MESH_ID = pl.DeviceIdType.MESH
QUARTERS = 4


class Sums:
    def __init__(self, index, p, far, total, send, recv):
        z = lax.axis_index("tensor")
        self.index, self.p, self.far, self.total, self.send, self.recv = index, p, far, total, send, recv
        self.middle = (z == 1) | (z == 2)
        self.end = (z == 0) | (z == 3)
        self.near = jnp.where(z == 0, 1, 2)
        self.mate = 3 - z
        self.edge = jnp.where(z == 1, 0, 3)

    def rows(self, c):
        return pl.ds(pl.multiple_of(c * AR_ROWS, AR_ROWS), AR_ROWS)

    def copy(self, s, d, kind_s, kind_r, c, to):
        r = self.rows(c)
        return pltpu.make_async_remote_copy(
            src_ref=s.at[r, :], dst_ref=d.at[r, :], send_sem=self.send.at[self.index, kind_s, c],
            recv_sem=self.recv.at[self.index, kind_r, c], device_id={"tensor": to}, device_id_type=MESH_ID)

    def out(self, c):
        return self.copy(self.p, self.far, 0, 0, c, self.near)

    def across(self, c):
        return self.copy(self.p, self.total, 0, 1, c, self.mate)

    def back(self, c):
        return self.copy(self.total, self.total, 1, 1, c, self.edge)

    def start(self, c):
        pl.when(self.end)(lambda: self.out(c).start())

    def mid(self, c):
        @pl.when(self.middle)
        def _():
            r = self.rows(c)
            self.out(c).wait_recv()
            self.p[r, :] = (self.p[r, :].astype(F32) + self.far[r, :].astype(F32)).astype(BF)
            self.across(c).start()

    def tot(self, c, then=None):
        @pl.when(self.middle)
        def _():
            r = self.rows(c)
            self.across(c).wait_recv()
            self.total[r, :] = (self.p[r, :].astype(F32) + self.total[r, :].astype(F32)).astype(BF)
            self.back(c).start()
            if then is not None:
                then(c)

    def got(self, c, then=None):
        @pl.when(self.end)
        def _():
            self.back(c).wait_recv()
            if then is not None:
                then(c)

    def finish(self, c):
        pl.when(self.end)(lambda: self.out(c).wait_send())

        @pl.when(self.middle)
        def _():
            self.across(c).wait_send()
            self.back(c).wait_send()


class Scatter:
    def __init__(self, job, gw, rx, send, recv, credit):
        d = lax.axis_index("dp")
        self.job, self.gw, self.rx, self.send, self.recv, self.credit = job, gw, rx, send, recv, credit
        self.core, self.x, self.y = lax.rem(d, 2), lax.rem(d // 2, 2), d // 4
        self.by_core = self.y * 4 + self.x * 2 + (1 - self.core)
        self.by_x = self.y * 4 + (1 - self.x) * 2 + self.core
        self.by_y = (1 - self.y) * 4 + self.x * 2 + self.core

    def copy(self, stage, h, s, d, to):
        return pltpu.make_async_remote_copy(
            src_ref=s, dst_ref=d, send_sem=self.send.at[self.job, stage, h], recv_sem=self.recv.at[self.job, stage, h],
            device_id={"dp": to}, device_id_type=MESH_ID)

    def cols(self, h):
        half = self.gw.shape[-1] // 2
        return pl.ds(h * half, half)

    def c0(self, h):
        return self.copy(0, h, self.gw.at[:, :, 1 - self.core, :, self.cols(h)], self.rx.at[0:2, :, :, self.cols(h)], self.by_core)

    def c1(self, h):
        to = self.rx.at[2, :, :, self.cols(h)]
        if h == 0:
            return self.copy(1, h, self.gw.at[:, 1 - self.x, self.core, :, self.cols(h)], to, self.by_x)
        return self.copy(1, h, self.gw.at[1 - self.y, :, self.core, :, self.cols(h)], to, self.by_y)

    def c2(self, h):
        to = self.rx.at[3, 0, :, self.cols(h)]
        if h == 0:
            return self.copy(2, h, self.gw.at[1 - self.y, self.x, self.core, :, self.cols(h)], to, self.by_y)
        return self.copy(2, h, self.gw.at[self.y, 1 - self.x, self.core, :, self.cols(h)], to, self.by_x)

    def begin(self, h):
        self.c0(h).start()

    def add(self, h):
        self.c0(h).wait_recv()
        c = self.cols(h)
        for y in range(2):
            for x in range(2):
                v = self.gw[y, x, self.core, :, c].astype(F32) + self.rx[y, x, :, c].astype(F32)
                self.gw[y, x, self.core, :, c] = v.astype(BF)
        self.c1(h).start()

    def second(self, h):
        self.c1(h).wait_recv()
        c = self.cols(h)
        for i in range(2):
            y, x = (i, self.x) if h == 0 else (self.y, i)
            v = self.gw[y, x, self.core, :, c].astype(F32) + self.rx[2, i, :, c].astype(F32)
            self.gw[y, x, self.core, :, c] = v.astype(BF)
        self.c2(h).start()

    def last(self, h):
        self.c2(h).wait_recv()
        c = self.cols(h)
        return self.gw[self.y, self.x, self.core, :, c].astype(F32) + self.rx[3, 0, :, c].astype(F32)

    def sent(self):
        for h in range(2):
            self.c0(h).wait_send()
            self.c1(h).wait_send()
            self.c2(h).wait_send()

    def give(self):
        for to in (self.by_core, self.by_x, self.by_y):
            pl.semaphore_signal(self.credit, inc=1, device_id={"dp": to}, device_id_type=MESH_ID)

    def take(self):
        pl.semaphore_wait(self.credit, 3)


def layer_kernel(
    n_images, fused, dp,
    len_ref, g1, b1, g2, b2, bup, bd,
    x_h, cot_h, wq_h, wk_h, wv_h, wo_h, wu_h, wd_h,
    out_h, gi_h, gu_o, gd_o, go_o, gq_o, gk_o, gv_o, vec_o,
    x, cot, wq, wk, wv, wo, wu, wd,
    n1, pq, pk, va, rd, at, al, st, mid, n2, hid, gu, pn, pd, far, tot, tot2,
    gwb, rxa, rxb, og, ogd, vec, rv,
    in_sem, out_sem, og_sem, zs, zr, ss, sr, vs, vr, credit,
):
    width = cot.shape[1]
    blocks = cot.shape[0] // BLK
    tiles = width // BLK
    z = lax.axis_index("tensor")
    d = lax.axis_index("dp")
    loads = [(x_h, x), (wq_h, wq), (wk_h, wk), (wv_h, wv), (wo_h, wo), (wu_h, wu), (cot_h, cot), (wd_h, wd)]
    loads = [pltpu.make_async_copy(s, t, in_sem.at[i]) for i, (s, t) in enumerate(loads)]
    for c in loads:
        c.start()
    first = Sums(0, pn, far, tot, zs, zr)
    second = Sums(1, pd, far, tot2, zs, zr)
    barrier = pltpu.get_barrier_semaphore()
    if fused:
        for k in range(1, dp):
            pl.semaphore_signal(barrier, inc=1, device_id={"dp": lax.rem(d + k, dp)}, device_id_type=MESH_ID)

    @pl.when(first.end)
    def _():
        pl.semaphore_signal(barrier, inc=1, device_id={"tensor": first.near}, device_id_type=MESH_ID)

    @pl.when(first.middle)
    def _():
        pl.semaphore_signal(barrier, inc=1, device_id={"tensor": first.mate}, device_id_type=MESH_ID)
        pl.semaphore_signal(barrier, inc=1, device_id={"tensor": first.edge}, device_id_type=MESH_ID)

    ends = ends_of(len_ref, n_images)
    m0, m1 = head_masks()
    ones = jnp.ones((BLK, PAIR), BF)
    diagonal = block_diagonal()
    vec[...] = jnp.zeros_like(vec)
    once = jnp.where(z == 1, 1.0, 0.0)
    matrix = lambda ref: ref[...].reshape(width, width)
    lanes_of = lambda ref, cols: ref[..., cols].reshape(width, BLK)

    jobs = {}
    slots = ((x, rxa), (gwb, rxb), (wu, wd))
    plan = (("up", n2, gu, gu_o), ("down", cot, hid, gd_o), ("out", at, cot, go_o), ("query", n1, rd, gq_o),
            ("key", n1, al, gk_o), ("value", n1, va, gv_o))
    for i, (name, l, r, o) in enumerate(plan):
        gw, rx = slots[i % 3]
        jobs[name] = (i, l, r, o, Scatter(i, gw, rx, ss, sr, credit.at[i % 3]))

    def gradient(name, half):
        i, l, r, o, s = jobs[name]
        for c in range(half * tiles // 2, (half + 1) * tiles // 2):
            cols = slice(c * BLK, (c + 1) * BLK)
            s.gw[..., cols] = tn(l[...], r[:, cols]).astype(BF).reshape(s.gw.shape[:-1] + (BLK,))
        if fused:
            s.begin(half)
        elif half == 1:
            for y in range(2):
                for x_ in range(2):
                    for k in range(2):
                        row = (y * 4 + x_ * 2 + k) * (width // 8)
                        pltpu.make_async_copy(s.gw.at[y, x_, k], o.at[pl.ds(row, width // 8), :], og_sem.at[0]).start()
                        pltpu.make_async_copy(s.gw.at[y, x_, k], o.at[pl.ds(row, width // 8), :], og_sem.at[0]).wait()

    def ready(name):
        if fused:
            jobs[name][4].take()

    def add(name):
        if fused:
            for h in range(2):
                jobs[name][4].add(h)

    def stage(name):
        if fused:
            for h in range(2):
                jobs[name][4].second(h)

    OG = {"up": 0, "out": 0, "query": 1, "key": 0, "value": 1}

    def out_copy(name):
        i, l, r, o, s = jobs[name]
        return pltpu.make_async_copy(ogd if name == "down" else og.at[OG[name]], o, og_sem.at[i])

    def last(name):
        if not fused:
            return
        i, l, r, o, s = jobs[name]
        half = width // 2
        earlier = {"out": "up", "key": "out", "value": "query"}.get(name)
        if earlier:
            out_copy(earlier).wait()
        for h in range(2):
            v = s.last(h)
            if name == "down":
                ogd[h * half:(h + 1) * half, :] = v.T
            else:
                og[OG[name], :, h * half:(h + 1) * half] = v
        out_copy(name).start()
        s.sent()
        if i < 3:
            s.give()

    for i in range(4):
        loads[i].wait()

    def forward_block(b, _):
        rows = pl.ds(pl.multiple_of(b * BLK, BLK), BLK)
        xb = x[b // 2, lax.rem(b, 2)].reshape(BLK, width).astype(F32)
        hat, _ = normed(xb)
        n1b = (hat * g1[...] + b1[...]).astype(BF)
        n1[rows, :] = n1b
        pq[rows, :] = feature(nn(n1b, wq[...]).astype(BF).astype(F32)).astype(BF)
        pk[rows, :] = feature(nn(n1b, wk[...]).astype(BF).astype(F32)).astype(BF)
        va[rows, :] = nn(n1b, wv[...]).astype(BF)
        down, _, cont, trail = block_masks(b, ends)
        down2 = two(down)
        for p in range(width // PAIR):
            lanes = slice(p * PAIR, (p + 1) * PAIR)
            q, k, v = pq[rows, lanes], pk[rows, lanes], va[rows, lanes]
            a = nt(jnp.concatenate([q * m0, q * m1], axis=0), k).astype(BF) * down2
            o = nn(a[:BLK], jnp.concatenate([v * m0, ones * m0], axis=1))
            o = o + nn(a[BLK:], jnp.concatenate([v * m1, ones * m1], axis=1))
            before = jnp.where(b > 0, st[jnp.maximum(b - 1, 0), p].astype(F32), 0.0).astype(BF)
            o = o + nn(q * cont, before)
            st[b, p] = (tn(k * trail, jnp.concatenate([v, ones], axis=1)) * diagonal).astype(BF)
            inverse = 1.0 / o[:, PAIR:]
            rd[rows, lanes] = inverse.astype(BF)
            attended = o[:, :PAIR] * inverse
            attended_low = attended.astype(BF)
            at[rows, lanes] = attended_low
            al[rows, lanes] = (attended - attended_low.astype(F32)).astype(BF)

        @pl.when(b == 0)
        def _():
            for i in range(4, 8):
                loads[i].wait()
            count = (dp - 1) if fused else 0
            pl.when(first.end)(lambda: pl.semaphore_wait(barrier, count + 1))
            pl.when(first.middle)(lambda: pl.semaphore_wait(barrier, count + 2))

        pl.when(b >= 2)(lambda: first.mid(b - 1))
        pl.when(b == 3)(lambda: first.tot(1))
        middle = xb + nn(at[rows, :], wo[...])
        mid[rows, :] = middle
        hat2, _ = normed(middle)
        n2b = (hat2 * g2[...] + b2[...]).astype(BF)
        n2[rows, :] = n2b
        cb = cot[rows, :]
        vec[0:1, :] += jnp.sum(cb.astype(F32), axis=0, keepdims=True)
        for c in range(tiles):
            cols = slice(c * BLK, (c + 1) * BLK)
            u = nn(n2b, lanes_of(wu, cols)) + bup[:, cols]
            gh = nt(cb, wd[c].reshape(BLK, width))
            th = jnp.tanh(C0 * (u + C1 * u * u * u))
            hid[rows, cols] = (0.5 * u * (1.0 + th)).astype(BF)
            slope = 0.5 * (1.0 + th) + 0.5 * u * (1.0 - th * th) * (C0 * (1.0 + 3.0 * C1 * u * u))
            gub = (gh * slope).astype(BF)
            gu[rows, cols] = gub
            vec[1:2, cols] += jnp.sum(gub.astype(F32), axis=0, keepdims=True)
        pn[rows, :] = nt(gu[rows, :], matrix(wu)).astype(BF)

        first.start(2 * b)
        first.start(2 * b + 1)
        pd[rows, :] = (nn(hid[rows, :], matrix(wd)) + once * (middle + bd[...])).astype(BF)
        pl.when(b == 1)(lambda: first.mid(0))
        pl.when(b == 2)(lambda: first.tot(0))
        pl.when(b == 3)(lambda: first.mid(3))
        return 0

    lax.fori_loop(0, blocks, forward_block, 0)
    if fused:
        jobs["out"][4].give()
    gradient("up", 0)
    gradient("up", 1)
    first.tot(2)
    gradient("down", 0)
    add("up")
    first.mid(4)
    gradient("down", 1)
    first.tot(3)

    def reload(b, k):
        return pltpu.make_async_copy(x_h.at[b // 2, lax.rem(b, 2), k],
                                     hid.at[pl.ds(pl.multiple_of(b * BLK + k * PAIR, PAIR), PAIR), :], in_sem.at[2 * b + k])

    for b in range(blocks):
        for k in range(2):
            reload(b, k).start()

    row = lax.broadcasted_iota(jnp.int32, (2 * PAIR, 2 * PAIR), 0) // HEAD
    lane = lax.broadcasted_iota(jnp.int32, (2 * PAIR, 2 * PAIR), 1) // HEAD
    same_head = jnp.where(row == lane, 1.0, 0.0).astype(BF)
    half = lax.rem(lax.broadcasted_iota(jnp.int32, (1, BLK), 1), HEAD) < HEAD // 2

    def norm_block(b):
        rows = pl.ds(pl.multiple_of(b * BLK, BLK), BLK)
        first.got(2 * b)
        first.got(2 * b + 1)
        hat, scale = normed(mid[rows, :])
        e = tot[rows, :].astype(F32)
        vec[2:3, :] += jnp.sum(e * hat, axis=0, keepdims=True)
        vec[3:4, :] += jnp.sum(e, axis=0, keepdims=True)
        gm = cot[rows, :].astype(F32) + norm_back(e, hat, scale, g2[...])
        mid[rows, :] = gm
        gbb = gm.astype(BF)
        cot[rows, :] = gbb
        ga = nt(gbb, wo[...])
        n = (ga * rd[rows, :].astype(F32)).astype(BF)
        prod = n.astype(F32) * (at[rows, :].astype(F32) + al[rows, :].astype(F32))
        rd[rows, :] = n
        high = prod.astype(BF)
        rest = (prod - high.astype(F32)).astype(BF)
        for c in range(tiles):
            cols = slice(c * BLK, (c + 1) * BLK)
            m = (nn(high[:, cols], same_head) + nn(rest[:, cols], same_head)) * (-2.0 / HEAD)
            m_high = m.astype(BF).astype(F32)
            al[rows, cols] = jnp.where(half, m_high, m - m_high).astype(BF)

    emit = lambda c: pltpu.make_async_copy(tot2.at[second.rows(c), :], out_h.at[second.rows(c), :], out_sem.at[0, c]).start()

    def core_block(b, middle_step):
        rows = pl.ds(pl.multiple_of(b * BLK, BLK), BLK)
        after_b = jnp.minimum(b + 1, blocks - 1)
        after_rows = pl.ds(pl.multiple_of(after_b * BLK, BLK), BLK)
        low, up, cont, trail = block_masks(b, ends)
        more = jnp.where(b < blocks - 1, 1.0, 0.0)
        cont_after = (block_masks(after_b, ends)[2].astype(F32) * more).astype(BF)
        low2, up2 = two(low), two(up)
        for p in range(width // PAIR):
            lanes = slice(p * PAIR, (p + 1) * PAIR)
            q, k, v = pq[rows, lanes], pk[rows, lanes], va[rows, lanes]
            n, m = rd[rows, lanes], al[rows, lanes]
            nm_after = jnp.concatenate([rd[after_rows, lanes], al[after_rows, lanes]], axis=1)
            after = (tn(pq[after_rows, lanes] * cont_after, nm_after) * diagonal).astype(BF)
            q0, q1, k0, k1, n0, n1_ = q * m0, q * m1, k * m0, k * m1, n * m0, n * m1
            nm = jnp.concatenate([n, m], axis=1)
            nm2 = jnp.concatenate(
                [jnp.concatenate([n0, m * m0], axis=1), jnp.concatenate([n1_, m * m1], axis=1)], axis=0
            )
            v1 = jnp.concatenate([v, ones], axis=1)
            v2 = jnp.concatenate(
                [jnp.concatenate([v * m0, ones * m0], axis=1), jnp.concatenate([v * m1, ones * m1], axis=1)], axis=0
            )
            da = nt(nm2, v1).astype(BF) * low2
            dat = nt(v2, nm).astype(BF) * up2
            a_t = nt(jnp.concatenate([k0, k1], axis=0), q).astype(BF) * up2
            before = jnp.where(b > 0, st[jnp.maximum(b - 1, 0), p].astype(F32), 0.0).astype(BF)
            dq = nn(da[:BLK], k0) + nn(da[BLK:], k1) + nt(nm * cont, before)
            dk = nn(dat[:BLK], q0) + nn(dat[BLK:], q1) + nt(v1 * trail, after)
            dv = nn(a_t[:BLK], n0) + nn(a_t[BLK:], n1_) + nn(k * trail, after[:, :PAIR])
            rd[rows, lanes] = (dq * jnp.minimum(q.astype(F32), 1.0)).astype(BF)
            al[rows, lanes] = (dk * jnp.minimum(k.astype(F32), 1.0)).astype(BF)
            va[rows, lanes] = dv.astype(BF)
            if p == width // PAIR // 2 - 1:
                middle_step()
        e = nt(rd[rows, :], wq[...]) + nt(al[rows, :], wk[...]) + nt(va[rows, :], wv[...])
        for k in range(2):
            reload(b, k).wait()
        hat, scale = normed(hid[rows, :].astype(F32))
        vec[4:5, :] += jnp.sum(e * hat, axis=0, keepdims=True)
        vec[5:6, :] += jnp.sum(e, axis=0, keepdims=True)
        mid[rows, :] = mid[rows, :] + norm_back(e, hat, scale, g1[...])
        pltpu.make_async_copy(mid.at[rows, :], gi_h.at[rows, :], out_sem.at[1, b]).start()

    def at_step(j, k, *acts):
        @pl.when(j == k)
        def _():
            for act in acts:
                act()

    def backward_step(j, _):
        at_step(j, 1, lambda: stage("up"), lambda: add("down"))
        at_step(j, 2, lambda: last("up"), lambda: stage("down"))

        @pl.when(j < blocks)
        def _():
            norm_block(j)

        at_step(j, 0, lambda: first.mid(5), lambda: first.tot(4))
        at_step(j, 2, *[functools.partial(second.start, c) for c in range(4)])
        at_step(j, 3, *[functools.partial(second.start, c) for c in range(4, 8)])
        at_step(j, 3, lambda: last("down"))
        at_step(j, 4, lambda: ready("out"), lambda: gradient("out", 0), lambda: gradient("out", 1))

        def middle_step():
            at_step(j, 1, lambda: first.mid(6), lambda: first.tot(5))
            at_step(j, 2, lambda: first.tot(7), lambda: second.mid(0))
            at_step(j, 3, lambda: second.mid(2), lambda: second.tot(1, emit))
            at_step(j, 4, lambda: second.mid(4), lambda: second.tot(3, emit), lambda: add("out"))

        @pl.when(j > 0)
        def _():
            core_block(j - 1, middle_step)

        at_step(j, 1, lambda: first.mid(7), lambda: first.tot(6))
        at_step(j, 2, lambda: second.mid(1), lambda: second.tot(0, emit))
        at_step(j, 3, lambda: second.mid(3), lambda: second.tot(2, emit))
        at_step(j, 4, lambda: second.mid(5), lambda: second.tot(4, emit), lambda: stage("out"))
        return 0

    lax.fori_loop(0, blocks + 1, backward_step, 0)
    if fused:
        own = pl.ds(pl.multiple_of(d * (width // dp), width // dp), width // dp)
        small = []
        for k in range(1, dp):
            to = lax.rem(d + k, dp)
            cols = pl.ds(pl.multiple_of(to * (width // dp), width // dp), width // dp)
            small.append(pltpu.make_async_remote_copy(
                src_ref=vec.at[:, cols], dst_ref=rv.at[k], send_sem=vs.at[k], recv_sem=vr.at[k],
                device_id={"dp": to}, device_id_type=MESH_ID))
        for c in small:
            c.start()
    ready("query")
    gradient("query", 0)
    gradient("query", 1)
    last("out")
    ready("key")
    gradient("key", 0)
    add("query")
    gradient("key", 1)
    second.mid(6)
    second.tot(5, emit)
    ready("value")
    gradient("value", 0)
    add("key")
    gradient("value", 1)
    stage("query")
    add("value")
    second.mid(7)
    second.tot(6, emit)
    last("query")
    stage("key")
    if fused:
        total = vec[:, own]
        for c in small:
            c.wait_recv()
        for k in range(1, dp):
            total = total + rv[k]
        vec_o[...] = total
        for c in small:
            c.wait_send()
    else:
        vec_o[...] = vec[...]
    for c in range(6):
        second.got(c, emit)
    second.tot(7, emit)
    last("key")
    stage("value")
    second.got(6, emit)
    second.got(7, emit)
    last("value")
    for c in range(8):
        first.finish(c)
        second.finish(c)
        pltpu.make_async_copy(tot2.at[second.rows(c), :], out_h.at[second.rows(c), :], out_sem.at[0, c]).wait()
    for b in range(blocks):
        rows = pl.ds(b * BLK, BLK)
        pltpu.make_async_copy(mid.at[rows, :], gi_h.at[rows, :], out_sem.at[1, b]).wait()
    if fused:
        for name in ("down", "key", "value"):
            out_copy(name).wait()


def per_device(dp, inputs, cotangent, lengths, ln1_gain, ln1_bias, w_query, w_key, w_value, w_out, ln2_gain, ln2_bias, w_up, b_up,
               w_down, b_down):
    tokens, width = inputs.shape
    n_images = lengths.shape[1]
    fused = dp == 8
    blocks, pairs = tokens // BLK, width // PAIR
    shape = jax.ShapeDtypeStruct
    full = shape((tokens, width), BF)
    piece, square = shape((width // dp, width), F32), shape((width, width), BF)
    anyspace = pl.BlockSpec(memory_space=pl.ANY)
    vmem = pl.BlockSpec(memory_space=VM)
    smem = pl.BlockSpec(memory_space=pltpu.SMEM)
    row = lambda v: v.reshape(1, -1)
    big = lambda dtype=BF: VM((tokens, width), dtype)
    weight = VM((width, width), BF)
    split = (2, 2, 2, width // 8, width)
    boxed = VM(split, BF)
    received = VM((4, 2, width // 8, width), BF)
    dma = pltpu.SemaphoreType.DMA
    if fused:
        weights_out = [piece, shape((width, width // dp), F32)] + [piece] * 4
    else:
        weights_out = [square] * 6
    outs = pl.pallas_call(
        functools.partial(layer_kernel, n_images, fused, dp),
        out_shape=[full, shape((tokens, width), F32)] + weights_out + [shape((8, width // dp if fused else width), F32)],
        in_specs=[smem] + [vmem] * 6 + [anyspace] * 8,
        out_specs=[anyspace] * 8 + [vmem],
        scratch_shapes=[boxed, big()] + [weight] * 4 + [boxed, received] + [big()] * 7
        + [VM((blocks, pairs, PAIR, 2 * PAIR), BF), big(F32)] + [big()] * 8
        + [boxed, received, received, VM((2, width // 8, width), F32), VM((width, width // 8), F32), VM((8, width), F32),
           VM((8, 8, width // 8), F32)]
        + [dma((8,)), dma((2, 8)), dma((6,)), dma((2, 2, 8)), dma((2, 2, 8)), dma((6, 3, 2)), dma((6, 3, 2)), dma((8,)), dma((8,)),
           pltpu.SemaphoreType.REGULAR((3,))],
        compiler_params=pltpu.CompilerParams(vmem_limit_bytes=VMEM_LIMIT, collective_id=0, has_side_effects=True),
    )(lengths, row(ln1_gain), row(ln1_bias), row(ln2_gain), row(ln2_bias), row(b_up), row(b_down),
      inputs.reshape(split), cotangent, w_query, w_key, w_value, w_out, w_up.reshape(split), w_down.reshape(4, 2, width // 8, width))
    out, gi, gu, gd, go, gq, gk, gv, vec = outs
    if not fused:
        scatter = lambda v, axis=0: lax.psum_scatter(v, "dp", scatter_dimension=axis, tiled=True)
        gu, go, gq, gk, gv = (scatter(v).astype(F32) for v in (gu, go, gq, gk, gv))
        gd = scatter(gd).astype(F32).T
        vec = scatter(vec, 1)
    return (out, gi, vec[4], vec[5], gq, gk, gv, go, vec[2], vec[3], gu, vec[1], gd, vec[0])


VMEM_LIMIT = 64 << 20


def solution(mesh):
    rows, whole = P("dp", None), P()
    placed = (rows, rows, rows) + (whole,) * 8 + (P(None, "tensor"), P("tensor"), P("tensor", None), whole)
    return jax.shard_map(
        functools.partial(per_device, mesh.shape["dp"]),
        mesh=mesh,
        in_specs=placed,
        out_specs=(rows, rows, P("dp"), P("dp"), rows, rows, rows, rows, P("dp"), P("dp"), P("dp", "tensor"),
                   P(("tensor", "dp")), P("tensor", "dp"), P("dp")),
        check_vma=False,
    )
```

```python
import functools

import jax
import jax.numpy as jnp
from jax import lax
from jax.experimental import pallas as pl
from jax.experimental.pallas import tpu as pltpu
from jax.sharding import PartitionSpec as P

EPS = 1e-05
BLK = 256
PAIR = 128
HEAD = 64
C0 = 0.7978845608028654
C1 = 0.044715
F32 = jnp.float32
BF = jnp.bfloat16
VM = pltpu.VMEM


def nn(a, b):
    return lax.dot_general(a, b, (((1,), (0,)), ((), ())), preferred_element_type=F32)


def nt(a, b):
    return lax.dot_general(a, b, (((1,), (1,)), ((), ())), preferred_element_type=F32)


def tn(a, b):
    return lax.dot_general(a, b, (((0,), (0,)), ((), ())), preferred_element_type=F32)


def mean(v):
    return jnp.mean(v, axis=-1, keepdims=True)


def normed(v):
    centered = v - mean(v)
    scale = lax.rsqrt(mean(centered * centered) + EPS)
    return centered * scale, scale


def norm_back(e, hat, scale, gain):
    eg = e * gain
    return scale * (eg - mean(eg) - hat * mean(eg * hat))


def feature(v):
    return jnp.where(v > 0, v + 1.0, jnp.exp(jnp.minimum(v, 0.0)))


def ends_of(len_ref, n_images):
    ends, total = [], 0
    for i in range(n_images):
        total = total + len_ref[0, i]
        ends.append(total)
    return ends


def segment_of(places, ends):
    seg = jnp.zeros(places.shape, jnp.int32)
    for end in ends:
        seg = seg + jnp.where(places >= end, 1, 0)
    return seg


def scalar_segment(place, ends):
    seg = 0
    for end in ends:
        seg = seg + jnp.where(place >= end, 1, 0)
    return seg


def head_masks():
    lane = lax.broadcasted_iota(jnp.int32, (1, PAIR), 1)
    first = jnp.where(lane < HEAD, 1.0, 0.0).astype(BF)
    return first, (1.0 - first.astype(F32)).astype(BF)


def block_diagonal():
    row = lax.broadcasted_iota(jnp.int32, (PAIR, 2 * PAIR), 0)
    lane = lax.broadcasted_iota(jnp.int32, (PAIR, 2 * PAIR), 1)
    return jnp.where((row < HEAD) == (lax.rem(lane, PAIR) < HEAD), 1.0, 0.0)


def block_masks(b, ends):
    col = segment_of(b * BLK + lax.broadcasted_iota(jnp.int32, (BLK, 1), 0), ends)
    row = segment_of(b * BLK + lax.broadcasted_iota(jnp.int32, (1, BLK), 1), ends)
    before = jnp.where(b > 0, scalar_segment(b * BLK - 1, ends), -1)
    last = scalar_segment(b * BLK + BLK - 1, ends)
    t = lax.broadcasted_iota(jnp.int32, (BLK, BLK), 0)
    s = lax.broadcasted_iota(jnp.int32, (BLK, BLK), 1)
    same = col == row
    down = jnp.where(same & (t >= s), 1.0, 0.0).astype(BF)
    up = jnp.where(same & (t <= s), 1.0, 0.0).astype(BF)
    cont = jnp.where(col == before, 1.0, 0.0).astype(BF)
    trail = jnp.where(col == last, 1.0, 0.0).astype(BF)
    return down, up, cont, trail


def two(v):
    return jnp.concatenate([v, v], axis=0)


EVEN = (128,) * 8
TAPERED = (128,) * 7 + (64, 32, 32)
MESH_ID = pl.DeviceIdType.MESH
QUARTERS = 4


class Sums:
    def __init__(self, index, p, far, total, send, recv, sizes):
        z = lax.axis_index("tensor")
        self.sizes, self.starts = sizes, [sum(sizes[:i]) for i in range(len(sizes))]
        self.index, self.p, self.far, self.total, self.send, self.recv = index, p, far, total, send, recv
        self.middle = (z == 1) | (z == 2)
        self.end = (z == 0) | (z == 3)
        self.near = jnp.where(z == 0, 1, 2)
        self.mate = 3 - z
        self.edge = jnp.where(z == 1, 0, 3)

    def rows(self, c):
        if isinstance(c, int):
            return pl.ds(self.starts[c], self.sizes[c])
        return pl.ds(pl.multiple_of(c * self.sizes[0], self.sizes[0]), self.sizes[0])

    def copy(self, s, d, kind_s, kind_r, c, to):
        r = self.rows(c)
        return pltpu.make_async_remote_copy(
            src_ref=s.at[r, :], dst_ref=d.at[r, :], send_sem=self.send.at[self.index, kind_s, c],
            recv_sem=self.recv.at[self.index, kind_r, c], device_id={"tensor": to}, device_id_type=MESH_ID)

    def out(self, c):
        return self.copy(self.p, self.far, 0, 0, c, self.near)

    def across(self, c):
        return self.copy(self.p, self.total, 0, 1, c, self.mate)

    def back(self, c):
        return self.copy(self.total, self.total, 1, 1, c, self.edge)

    def start(self, c):
        pl.when(self.end)(lambda: self.out(c).start())

    def mid(self, c):
        @pl.when(self.middle)
        def _():
            r = self.rows(c)
            self.out(c).wait_recv()
            self.p[r, :] = (self.p[r, :].astype(F32) + self.far[r, :].astype(F32)).astype(BF)
            self.across(c).start()

    def tot(self, c, then=None):
        @pl.when(self.middle)
        def _():
            r = self.rows(c)
            self.across(c).wait_recv()
            self.total[r, :] = (self.p[r, :].astype(F32) + self.total[r, :].astype(F32)).astype(BF)
            self.back(c).start()
            if then is not None:
                then(c)

    def got(self, c, then=None):
        @pl.when(self.end)
        def _():
            self.back(c).wait_recv()
            if then is not None:
                then(c)

    def finish(self, c):
        pl.when(self.end)(lambda: self.out(c).wait_send())

        @pl.when(self.middle)
        def _():
            self.across(c).wait_send()
            self.back(c).wait_send()


class Scatter:
    def __init__(self, job, gw, rx, send, recv, credit, width):
        d = lax.axis_index("dp")
        self.half = width // 2
        self.job, self.gw, self.rx, self.send, self.recv, self.credit = job, gw, rx, send, recv, credit
        self.core, self.x, self.y = lax.rem(d, 2), lax.rem(d // 2, 2), d // 4
        self.by_core = self.y * 4 + self.x * 2 + (1 - self.core)
        self.by_x = self.y * 4 + (1 - self.x) * 2 + self.core
        self.by_y = (1 - self.y) * 4 + self.x * 2 + self.core

    def copy(self, stage, h, s, d, to):
        return pltpu.make_async_remote_copy(
            src_ref=s, dst_ref=d, send_sem=self.send.at[self.job, stage, h], recv_sem=self.recv.at[self.job, stage, h],
            device_id={"dp": to}, device_id_type=MESH_ID)

    def cols(self, h):
        return pl.ds(h * self.half, self.half)

    def c0(self, h):
        return self.copy(0, h, self.gw.at[:, :, 1 - self.core, :, self.cols(h)], self.rx.at[0:2, :, :, self.cols(h)], self.by_core)

    def c1(self, h):
        to = self.rx.at[2, :, :, self.cols(h)]
        if h == 0:
            return self.copy(1, h, self.gw.at[:, 1 - self.x, self.core, :, self.cols(h)], to, self.by_x)
        return self.copy(1, h, self.gw.at[1 - self.y, :, self.core, :, self.cols(h)], to, self.by_y)

    def c2(self, h):
        to = self.rx.at[3, 0, :, self.cols(h)]
        if h == 0:
            return self.copy(2, h, self.gw.at[1 - self.y, self.x, self.core, :, self.cols(h)], to, self.by_y)
        return self.copy(2, h, self.gw.at[self.y, 1 - self.x, self.core, :, self.cols(h)], to, self.by_x)

    def begin(self, h):
        self.c0(h).start()

    def add(self, h):
        self.c0(h).wait_recv()
        c = self.cols(h)
        for y in range(2):
            for x in range(2):
                v = self.gw[y, x, self.core, :, c].astype(F32) + self.rx[y, x, :, c].astype(F32)
                self.gw[y, x, self.core, :, c] = v.astype(BF)
        self.c1(h).start()

    def second(self, h):
        self.c1(h).wait_recv()
        c = self.cols(h)
        for i in range(2):
            y, x = (i, self.x) if h == 0 else (self.y, i)
            v = self.gw[y, x, self.core, :, c].astype(F32) + self.rx[2, i, :, c].astype(F32)
            self.gw[y, x, self.core, :, c] = v.astype(BF)
        self.c2(h).start()

    def last(self, h):
        self.c2(h).wait_recv()
        c = self.cols(h)
        return self.gw[self.y, self.x, self.core, :, c].astype(F32) + self.rx[3, 0, :, c].astype(F32)

    def sent(self):
        for h in range(2):
            self.c0(h).wait_send()
            self.c1(h).wait_send()
            self.c2(h).wait_send()

    def give(self):
        for to in (self.by_core, self.by_x, self.by_y):
            pl.semaphore_signal(self.credit, inc=1, device_id={"dp": to}, device_id_type=MESH_ID)

    def take(self):
        pl.semaphore_wait(self.credit, 3)


def layer_kernel(
    n_images, fused, dp,
    len_ref, g1, b1, g2, b2, bup, bd,
    x_h, cot_h, wq_h, wk_h, wv_h, wo_h, wu_h, wd_h,
    out_h, gi_h, gu_o, gd_o, go_o, gq_o, gk_o, gv_o, vec_o,
    x, cot, wq, wk, wv, wo, wu, wd,
    n1, pq, pk, va, rd, at, al, st, mid, n2, hid, gu, pn, pd, far, tot, tot2,
    gwb, rxa, rxb, ogd, vec, rv,
    in_sem, out_sem, og_sem, zs, zr, ss, sr, vs, vr, credit,
):
    width = cot.shape[1]
    blocks = cot.shape[0] // BLK
    tiles = width // BLK
    z = lax.axis_index("tensor")
    d = lax.axis_index("dp")
    loads = [(x_h.at[0, 0], x.at[0, 0]), (wq_h, wq), (wk_h, wk), (wv_h, wv), (x_h.at[0, 1], x.at[0, 1]), (x_h.at[1], x.at[1]),
             (wo_h, wo), (wu_h, wu), (cot_h, cot), (wd_h, wd)]
    loads = [pltpu.make_async_copy(s, t, in_sem.at[i]) for i, (s, t) in enumerate(loads)]
    for c in loads[:4]:
        c.start()
    first = Sums(0, pn, far, tot, zs, zr, EVEN)
    second = Sums(1, pd, n2, tot2, zs, zr, TAPERED)
    barrier = pltpu.get_barrier_semaphore()
    if fused:
        for k in range(1, dp):
            pl.semaphore_signal(barrier, inc=1, device_id={"dp": lax.rem(d + k, dp)}, device_id_type=MESH_ID)

    @pl.when(first.end)
    def _():
        pl.semaphore_signal(barrier, inc=1, device_id={"tensor": first.near}, device_id_type=MESH_ID)

    @pl.when(first.middle)
    def _():
        pl.semaphore_signal(barrier, inc=1, device_id={"tensor": first.mate}, device_id_type=MESH_ID)
        pl.semaphore_signal(barrier, inc=1, device_id={"tensor": first.edge}, device_id_type=MESH_ID)

    ends = ends_of(len_ref, n_images)
    m0, m1 = head_masks()
    ones = jnp.ones((BLK, PAIR), BF)
    diagonal = block_diagonal()
    vec[...] = jnp.zeros_like(vec)
    once = jnp.where(z == 1, 1.0, 0.0)
    matrix = lambda ref: ref[...].reshape(width, width)
    apart = pl.when(z >= 0)

    def at_step(j, k, *acts):
        @pl.when(j == k)
        def _():
            for act in acts:
                act()

    def forward_block(b, _):
        rows = pl.ds(pl.multiple_of(b * BLK, BLK), BLK)
        at_step(b, 0, loads[0].wait)
        xb = x[b // 2, lax.rem(b, 2)].reshape(BLK, width).astype(F32)
        hat, _ = normed(xb)
        n1b = (hat * g1[...] + b1[...]).astype(BF)
        n1[:, rows] = n1b.T
        at_step(b, 0, loads[1].wait, loads[6].start, loads[7].start)
        pq[rows, :] = feature(nn(n1b, wq[...]).astype(BF).astype(F32)).astype(BF)
        at_step(b, 0, loads[2].wait, loads[8].start, loads[9].start, loads[4].start, loads[5].start)
        pk[rows, :] = feature(nn(n1b, wk[...]).astype(BF).astype(F32)).astype(BF)
        at_step(b, 0, loads[3].wait)
        va[rows, :] = nn(n1b, wv[...]).astype(BF)
        down, _, cont, trail = block_masks(b, ends)
        down2 = two(down)
        for p in range(width // PAIR):
            lanes = slice(p * PAIR, (p + 1) * PAIR)
            q, k, v = pq[rows, lanes], pk[rows, lanes], va[rows, lanes]
            a = nt(jnp.concatenate([q * m0, q * m1], axis=0), k).astype(BF) * down2
            o = nn(a[:BLK], jnp.concatenate([v * m0, ones * m0], axis=1))
            o = o + nn(a[BLK:], jnp.concatenate([v * m1, ones * m1], axis=1))
            before = jnp.where(b > 0, st[jnp.maximum(b - 1, 0), p].astype(F32), 0.0).astype(BF)
            o = o + nn(q * cont, before)
            st[b, p] = (tn(k * trail, jnp.concatenate([v, ones], axis=1)) * diagonal).astype(BF)
            inverse = 1.0 / o[:, PAIR:]
            rd[rows, lanes] = inverse.astype(BF)
            attended = o[:, :PAIR] * inverse
            attended_low = attended.astype(BF)
            at[rows, lanes] = attended_low
            al[rows, lanes] = (attended - attended_low.astype(F32)).astype(BF)

        @pl.when(b == 0)
        def _():
            count = (dp - 1) if fused else 0
            pl.when(first.end)(lambda: pl.semaphore_wait(barrier, count + 1))
            pl.when(first.middle)(lambda: pl.semaphore_wait(barrier, count + 2))
            for i in range(4, 8):
                loads[i].wait()

        at_step(b, 2, lambda: first.mid(1))
        at_step(b, 3, lambda: first.tot(1))
        middle = xb + nn(at[rows, :], wo[...])
        mid[rows, :] = middle
        hat2, _ = normed(middle)
        n2b = (hat2 * g2[...] + b2[...]).astype(BF)
        n2[:, rows] = n2b.T
        at_step(b, 0, loads[8].wait, loads[9].wait)
        cb = cot[rows, :]
        vec[0:1, :] += jnp.sum(cb.astype(F32), axis=0, keepdims=True)
        for c in range(tiles):
            cols = slice(c * BLK, (c + 1) * BLK)
            u = nn(n2b, wu[..., cols].reshape(width, BLK)) + bup[:, cols]
            gh = nt(cb, wd[c].reshape(BLK, width))
            th = jnp.tanh(C0 * (u + C1 * u * u * u))
            hid[rows, cols] = (0.5 * u * (1.0 + th)).astype(BF)
            slope = 0.5 * (1.0 + th) + 0.5 * u * (1.0 - th * th) * (C0 * (1.0 + 3.0 * C1 * u * u))
            gub = (gh * slope).astype(BF)
            gu[rows, cols] = gub
            vec[1:2, cols] += jnp.sum(gub.astype(F32), axis=0, keepdims=True)
        at_step(b, 1, lambda: first.mid(0))
        at_step(b, 2, lambda: first.tot(0))
        at_step(b, 3, lambda: first.mid(3))
        pn[rows, :] = nt(gu[rows, :], matrix(wu)).astype(BF)
        first.start(2 * b)
        first.start(2 * b + 1)
        pd[rows, :] = (nn(hid[rows, :], matrix(wd)) + once * (middle + bd[...])).astype(BF)
        at_step(b, 2, lambda: first.mid(2))
        at_step(b, 3, lambda: first.tot(2))
        return 0

    lax.fori_loop(0, blocks, forward_block, 0)

    groups = tiles
    jobs = {}
    slots = ((x, rxa), (gwb, rxb), (wu, wd))
    for i, name in enumerate(["up", "down", "out"] + list(range(groups))):
        gw, rx = slots[i % 3]
        jobs[name] = Scatter(i, gw, rx, ss, sr, credit.at[i % 3], 3 * BLK if i > 2 else width)
    last_job = 2 + groups

    def put(name, col, value):
        gw = jobs[name].gw
        gw[..., col:col + BLK] = value.astype(BF).reshape(gw.shape[:-1] + (BLK,))

    def send_whole(name, targets):
        gw = jobs[name].gw
        copies = []
        for y in range(2):
            for x_ in range(2):
                for k in range(2):
                    row = pl.ds((y * 4 + x_ * 2 + k) * (width // 8), width // 8)
                    for n, (o, col, o_col, wide) in enumerate(targets):
                        copies.append(pltpu.make_async_copy(gw.at[y, x_, k, :, col:col + wide], o.at[row, o_col:o_col + wide],
                                                            og_sem.at[0]))
        for c in copies:
            c.start()
            c.wait()

    def gradient(name, l, r, half):
        for c in range(half * tiles // 2, (half + 1) * tiles // 2):
            apart(lambda: put(name, c * BLK, nn(l[...], r[:, c * BLK:(c + 1) * BLK])))
        if fused:
            jobs[name].begin(half)
        elif half == 1:
            send_whole(name, [({"up": gu_o, "down": gd_o, "out": go_o}[name], 0, 0, width)])

    def projections(g):
        cols = slice(g * BLK, (g + 1) * BLK)
        apart(lambda: put(g, 0, nn(n1[...], rd[:, cols])))
        apart(lambda: put(g, BLK, nn(n1[...], al[:, cols])))
        if fused:
            jobs[g].begin(0)
        apart(lambda: put(g, 2 * BLK, nn(n1[...], va[:, cols])))
        if fused:
            jobs[g].begin(1)
        else:
            send_whole(g, [(o, i * BLK, g * BLK, BLK) for i, o in enumerate((gq_o, gk_o, gv_o))])

    def turn(ref):
        def part(c, _):
            rows = pl.ds(pl.multiple_of(c * BLK, BLK), BLK)
            gu[:, rows] = ref[rows, :].T
            return 0

        lax.fori_loop(0, blocks, part, 0)

    def ready(name):
        if fused:
            jobs[name].take()
            for c in out_copies({"out": None, 0: "up", 1: "down", 2: "out", 3: 0}[name]) if name != "out" else ():
                c.wait()

    def add(name):
        if fused:
            for h in range(2):
                jobs[name].add(h)

    def stage(name):
        if fused:
            for h in range(2):
                jobs[name].second(h)

    def out_copies(name):
        if name == "down":
            return [pltpu.make_async_copy(ogd, gd_o, og_sem.at[1])]
        s = jobs[name]
        mine = s.gw.at[s.y, s.x, s.core]
        if name in ("up", "out"):
            return [pltpu.make_async_copy(mine, gu_o if name == "up" else go_o, og_sem.at[s.job])]
        return [pltpu.make_async_copy(mine.at[:, i * BLK:(i + 1) * BLK], o.at[:, name * BLK:(name + 1) * BLK],
                                      og_sem.at[3 + 3 * name + i]) for i, o in enumerate((gq_o, gk_o, gv_o))]

    def last(name):
        if not fused:
            return
        s = jobs[name]
        for h in range(2):
            v = s.last(h)
            if name == "down":
                ogd[h * s.half:(h + 1) * s.half, :] = v.T.astype(BF)
            else:
                s.gw[s.y, s.x, s.core, :, s.cols(h)] = v.astype(BF)
        for c in out_copies(name):
            c.start()
        s.sent()
        if s.job + 3 <= last_job:
            s.give()

    if fused:
        jobs["out"].give()
    gradient("up", n2, gu, 0)
    gradient("up", n2, gu, 1)
    first.mid(4)
    turn(cot)
    gradient("down", gu, hid, 0)
    add("up")
    gradient("down", gu, hid, 1)
    first.tot(3)

    def reload(b, k):
        return pltpu.make_async_copy(x_h.at[b // 2, lax.rem(b, 2), k],
                                     hid.at[pl.ds(pl.multiple_of(b * BLK + k * PAIR, PAIR), PAIR), :], in_sem.at[2 * b + k])

    for b in range(blocks):
        for k in range(2):
            reload(b, k).start()

    row = lax.broadcasted_iota(jnp.int32, (2 * PAIR, 2 * PAIR), 0) // HEAD
    lane = lax.broadcasted_iota(jnp.int32, (2 * PAIR, 2 * PAIR), 1) // HEAD
    same_head = jnp.where(row == lane, 1.0, 0.0).astype(BF)
    half_lane = lax.rem(lax.broadcasted_iota(jnp.int32, (1, BLK), 1), HEAD) < HEAD // 2

    def norm_block(b):
        rows = pl.ds(pl.multiple_of(b * BLK, BLK), BLK)
        first.got(2 * b)
        first.got(2 * b + 1)
        hat, scale = normed(mid[rows, :])
        e = tot[rows, :].astype(F32)
        vec[2:3, :] += jnp.sum(e * hat, axis=0, keepdims=True)
        vec[3:4, :] += jnp.sum(e, axis=0, keepdims=True)
        gm = cot[rows, :].astype(F32) + norm_back(e, hat, scale, g2[...])
        mid[rows, :] = gm
        gbb = gm.astype(BF)
        cot[rows, :] = gbb
        ga = nt(gbb, wo[...])
        n = (ga * rd[rows, :].astype(F32)).astype(BF)
        prod = n.astype(F32) * (at[rows, :].astype(F32) + al[rows, :].astype(F32))
        rd[rows, :] = n
        high = prod.astype(BF)
        rest = (prod - high.astype(F32)).astype(BF)
        for c in range(tiles):
            cols = slice(c * BLK, (c + 1) * BLK)
            m = (nn(high[:, cols], same_head) + nn(rest[:, cols], same_head)) * (-2.0 / HEAD)
            m_high = m.astype(BF).astype(F32)
            al[rows, cols] = jnp.where(half_lane, m_high, m - m_high).astype(BF)

    emit = lambda c: pltpu.make_async_copy(tot2.at[second.rows(c), :], out_h.at[second.rows(c), :], out_sem.at[0, c]).start()

    def core_masks(b):
        after_b = jnp.minimum(b + 1, blocks - 1)
        low, up, cont, trail = block_masks(b, ends)
        more = jnp.where(b < blocks - 1, 1.0, 0.0)
        cont_after = (block_masks(after_b, ends)[2].astype(F32) * more).astype(BF)
        return two(low), two(up), cont, trail, cont_after

    def core_pair(b, p, masks):
        low2, up2, cont, trail, cont_after = masks
        rows = pl.ds(pl.multiple_of(b * BLK, BLK), BLK)
        after_rows = pl.ds(pl.multiple_of(jnp.minimum(b + 1, blocks - 1) * BLK, BLK), BLK)
        lanes = slice(p * PAIR, (p + 1) * PAIR)
        q, k, v = pq[rows, lanes], pk[rows, lanes], va[rows, lanes]
        n, m = rd[rows, lanes], al[rows, lanes]
        nm_after = jnp.concatenate([rd[after_rows, lanes], al[after_rows, lanes]], axis=1)
        after = (tn(pq[after_rows, lanes] * cont_after, nm_after) * diagonal).astype(BF)
        q0, q1, k0, k1, n0, n1_ = q * m0, q * m1, k * m0, k * m1, n * m0, n * m1
        nm = jnp.concatenate([n, m], axis=1)
        nm2 = jnp.concatenate(
            [jnp.concatenate([n0, m * m0], axis=1), jnp.concatenate([n1_, m * m1], axis=1)], axis=0
        )
        v1 = jnp.concatenate([v, ones], axis=1)
        v2 = jnp.concatenate(
            [jnp.concatenate([v * m0, ones * m0], axis=1), jnp.concatenate([v * m1, ones * m1], axis=1)], axis=0
        )
        da = nt(nm2, v1).astype(BF) * low2
        dat = nt(v2, nm).astype(BF) * up2
        a_t = nt(jnp.concatenate([k0, k1], axis=0), q).astype(BF) * up2
        before = jnp.where(b > 0, st[jnp.maximum(b - 1, 0), p].astype(F32), 0.0).astype(BF)
        dq = nn(da[:BLK], k0) + nn(da[BLK:], k1) + nt(nm * cont, before)
        dk = nn(dat[:BLK], q0) + nn(dat[BLK:], q1) + nt(v1 * trail, after)
        dv = nn(a_t[:BLK], n0) + nn(a_t[BLK:], n1_) + nn(k * trail, after[:, :PAIR])
        rd[rows, lanes] = (dq * jnp.minimum(q.astype(F32), 1.0)).astype(BF)
        al[rows, lanes] = (dk * jnp.minimum(k.astype(F32), 1.0)).astype(BF)
        va[rows, lanes] = dv.astype(BF)

    def input_block(b):
        rows = pl.ds(pl.multiple_of(b * BLK, BLK), BLK)
        e = nt(rd[rows, :], wq[...]) + nt(al[rows, :], wk[...]) + nt(va[rows, :], wv[...])
        for k in range(2):
            reload(b, k).wait()
        hat, scale = normed(hid[rows, :].astype(F32))
        vec[4:5, :] += jnp.sum(e * hat, axis=0, keepdims=True)
        vec[5:6, :] += jnp.sum(e, axis=0, keepdims=True)
        hid[rows, :] = (mid[rows, :] + norm_back(e, hat, scale, g1[...])).astype(BF)
        pltpu.make_async_copy(hid.at[rows, :], gi_h.at[rows, :], out_sem.at[1, b]).start()

    starts = lambda *pieces: [functools.partial(second.start, c) for c in pieces]

    def backward_step(j, _):
        at_step(j, 2, lambda: last("up"), lambda: stage("down"))
        apart(lambda: norm_block(j))
        at_step(j, 1, lambda: first.mid(5))

        @pl.when(j > 0)
        def _():
            masks = core_masks(j - 1)
            for p in range(width // PAIR):
                core_pair(j - 1, p, masks)
                if p == 0:
                    at_step(j, 2, lambda: first.tot(6), *starts(*range(4, len(TAPERED))))
                if p == 1:
                    at_step(j, 1, lambda: first.tot(4))
                if p == 2:
                    at_step(j, 1, lambda: stage("up"), lambda: add("down"))
                if p == 3:
                    at_step(j, 2, lambda: second.mid(0))
                if p == 4:
                    at_step(j, 1, lambda: first.mid(6), *starts(0, 1, 2, 3))
                if p == 6:
                    at_step(j, 2, lambda: first.tot(7))
                if p == 7:
                    at_step(j, 1, lambda: first.tot(5))
            apart(lambda: input_block(j - 1))

        at_step(j, 1, lambda: first.mid(7))
        at_step(j, 2, lambda: second.mid(1))
        return 0

    lax.fori_loop(0, blocks - 1, backward_step, 0)
    apart(lambda: norm_block(blocks - 1))
    ready("out")
    turn(at)
    gradient("out", gu, cot, 0)
    gradient("out", gu, cot, 1)
    last("down")
    second.tot(0, emit)

    def late_group(b, g):
        masks = core_masks(b)
        for p in (2 * g, 2 * g + 1):
            core_pair(b, p, masks)

    halfway = {
        0: (lambda: second.mid(2), lambda: add("out")),
        1: (lambda: second.mid(3), lambda: add(0), lambda: stage("out")),
        2: (lambda: add(1), lambda: stage(0), lambda: last("out")),
        3: (lambda: add(2), lambda: stage(1)),
    }
    before_sums = {
        2: (lambda: second.tot(3, emit),),
        3: (lambda: second.tot(4, emit), lambda: last(0)),
    }
    after_sums = {
        0: (lambda: second.tot(1, emit),),
        1: (lambda: second.mid(4), lambda: second.tot(2, emit)),
        2: (lambda: second.mid(5),),
        3: (lambda: second.mid(6), lambda: last(1)),
    }
    for g in range(groups):
        apart(functools.partial(late_group, blocks - 2, g))
        for act in halfway[g]:
            act()
        apart(functools.partial(late_group, blocks - 1, g))
        for act in before_sums.get(g, ()):
            act()
        ready(g)
        projections(g)
        for act in after_sums[g]:
            act()
    apart(lambda: input_block(blocks - 2))
    second.tot(5, emit)
    stage(2)
    add(3)
    apart(lambda: input_block(blocks - 1))
    second.mid(7)
    second.mid(8)
    second.mid(9)
    if fused:
        own = pl.ds(pl.multiple_of(d * (width // dp), width // dp), width // dp)
        small = []
        for k in range(1, dp):
            to = lax.rem(d + k, dp)
            cols = pl.ds(pl.multiple_of(to * (width // dp), width // dp), width // dp)
            small.append(pltpu.make_async_remote_copy(
                src_ref=vec.at[:, cols], dst_ref=rv.at[k], send_sem=vs.at[k], recv_sem=vr.at[k],
                device_id={"dp": to}, device_id_type=MESH_ID))
        for c in small:
            c.start()
    second.tot(6, emit)
    last(2)
    stage(3)
    second.tot(7, emit)
    second.tot(8, emit)
    second.tot(9, emit)
    if fused:
        total = vec[:, own]
        for c in small:
            c.wait_recv()
        for k in range(1, dp):
            total = total + rv[k]
        vec_o[...] = total
        for c in small:
            c.wait_send()
    else:
        vec_o[...] = vec[...]
    last(3)
    for c in range(len(TAPERED)):
        second.got(c, emit)
    for c in range(len(EVEN)):
        first.finish(c)
    for c in range(len(TAPERED)):
        second.finish(c)
        pltpu.make_async_copy(tot2.at[second.rows(c), :], out_h.at[second.rows(c), :], out_sem.at[0, c]).wait()
    for b in range(blocks):
        rows = pl.ds(b * BLK, BLK)
        pltpu.make_async_copy(hid.at[rows, :], gi_h.at[rows, :], out_sem.at[1, b]).wait()
    if fused:
        for name in (1, 2, 3):
            for c in out_copies(name):
                c.wait()


def finish_kernel(out_h, gi_h, *refs):
    weights, vec = refs[:6], refs[6]
    out_o, gi_o = refs[7:9]
    weights_o, vecs_o = refs[9:15], refs[15:21]
    narrow, wide, small, small_wide, tall, tall_wide, passed, sem_in, sem_out, sem = refs[21:]
    rows = gi_h.shape[0] // 8
    part = lambda c: pl.ds(c * rows, rows)
    ins = [pltpu.make_async_copy(gi_h.at[part(c), :], narrow.at[part(c), :], sem_in.at[c]) for c in range(8)]
    outs = [pltpu.make_async_copy(wide.at[part(c), :], gi_o.at[part(c), :], sem_out.at[c]) for c in range(8)]
    where = [(tall, tall_wide) if i == 1 else (small.at[i], small_wide.at[i]) for i in range(6)]
    ins += [pltpu.make_async_copy(weights[i], where[i][0], sem_in.at[8 + i]) for i in range(6)]
    outs += [pltpu.make_async_copy(where[i][1], weights_o[i], sem_out.at[8 + i]) for i in range(6)]
    for c in ins[:8]:
        c.start()
    for c in ins[8:]:
        c.start()
    through = [[pltpu.make_async_copy(s.at[part(c), :], t.at[part(c), :], sem.at[i, c])
                for i, (s, t) in enumerate(((out_h, passed), (passed, out_o)))] for c in range(8)]
    for c in through:
        c[0].start()
    for i, o in enumerate(vecs_o):
        o[...] = vec[i, :]
    for c in range(8):
        ins[c].wait()
        wide[part(c), :] = narrow[part(c), :].astype(F32)
        outs[c].start()
    for i in range(6):
        ins[8 + i].wait()
        where[i][1][...] = where[i][0][...].astype(F32)
        outs[8 + i].start()
    for c in through:
        c[0].wait()
        c[1].start()
    for c in outs:
        c.wait()
    for c in through:
        c[1].wait()


def per_device(dp, inputs, cotangent, lengths, ln1_gain, ln1_bias, w_query, w_key, w_value, w_out, ln2_gain, ln2_bias, w_up, b_up,
               w_down, b_down):
    tokens, width = inputs.shape
    n_images = lengths.shape[1]
    fused = dp == 8
    blocks, pairs = tokens // BLK, width // PAIR
    shape = jax.ShapeDtypeStruct
    full = shape((tokens, width), BF)
    piece, square = shape((width // dp, width), BF), shape((width, width), BF)
    tall = shape((width, width // dp), BF)
    anyspace = pl.BlockSpec(memory_space=pl.ANY)
    vmem = pl.BlockSpec(memory_space=VM)
    smem = pl.BlockSpec(memory_space=pltpu.SMEM)
    row = lambda v: v.reshape(1, -1)
    big = lambda dtype=BF: VM((tokens, width), dtype)
    weight = VM((width, width), BF)
    split = (2, 2, 2, width // 8, width)
    boxed = VM(split, BF)
    received = VM((4, 2, width // 8, width), BF)
    dma = pltpu.SemaphoreType.DMA
    weights_out = [piece, tall] + [piece] * 4 if fused else [square] * 6
    pieces = max(len(EVEN), len(TAPERED))
    outs = pl.pallas_call(
        functools.partial(layer_kernel, n_images, fused, dp),
        out_shape=[full, full] + weights_out + [shape((8, width // dp if fused else width), F32)],
        in_specs=[smem] + [vmem] * 6 + [anyspace] * 8,
        out_specs=[anyspace] * 8 + [vmem],
        scratch_shapes=[boxed, big()] + [weight] * 4 + [boxed, received] + [big()] * 7
        + [VM((blocks, pairs, PAIR, 2 * PAIR), BF), big(F32)] + [big()] * 8
        + [boxed, received, received, VM((width, width // 8), BF), VM((8, width), F32),
           VM((8, 8, width // 8), F32)]
        + [dma((10,)), dma((2, pieces)), dma((15,)), dma((2, 2, pieces)), dma((2, 2, pieces)), dma((7, 3, 2)), dma((7, 3, 2)),
           dma((8,)), dma((8,)), pltpu.SemaphoreType.REGULAR((3,))],
        compiler_params=pltpu.CompilerParams(vmem_limit_bytes=VMEM_LIMIT, collective_id=0, has_side_effects=True),
    )(lengths, row(ln1_gain), row(ln1_bias), row(ln2_gain), row(ln2_bias), row(b_up), row(b_down),
      inputs.reshape(split), cotangent, w_query, w_key, w_value, w_out, w_up.reshape(split), w_down.reshape(4, 2, width // 8, width))
    out, gi, gu, gd, go, gq, gk, gv, vec = outs
    if fused:
        wide = lambda s: shape(s.shape, F32)
        small = shape((width // dp,), F32)
        outs = pl.pallas_call(
            finish_kernel,
            out_shape=[full, wide(full)] + [wide(s) for s in weights_out] + [small] * 6,
            in_specs=[anyspace] * 8 + [vmem],
            out_specs=[anyspace] * 8 + [vmem] * 6,
            scratch_shapes=[big(), big(F32), VM((6,) + piece.shape, BF), VM((6,) + piece.shape, F32), VM(tall.shape, BF),
                            VM(tall.shape, F32), big(), dma((14,)), dma((14,)), dma((2, 8))],
            compiler_params=pltpu.CompilerParams(vmem_limit_bytes=VMEM_LIMIT),
        )(out, gi, gu, gd, go, gq, gk, gv, vec)
        out, gi, gu, gd, go, gq, gk, gv = outs[:8]
        vec = outs[8:]
    else:
        scatter = lambda v, axis=0: lax.psum_scatter(v, "dp", scatter_dimension=axis, tiled=True)
        gu, go, gq, gk, gv = (scatter(v).astype(F32) for v in (gu, go, gq, gk, gv))
        gd = scatter(gd).astype(F32).T
        vec = scatter(vec, 1)
        gi = gi.astype(F32)
    return (out, gi, vec[4], vec[5], gq, gk, gv, go, vec[2], vec[3], gu, vec[1], gd, vec[0])


VMEM_LIMIT = 64 << 20


def solution(mesh):
    rows, whole = P("dp", None), P()
    placed = (rows, rows, rows) + (whole,) * 8 + (P(None, "tensor"), P("tensor"), P("tensor", None), whole)
    return jax.shard_map(
        functools.partial(per_device, mesh.shape["dp"]),
        mesh=mesh,
        in_specs=placed,
        out_specs=(rows, rows, P("dp"), P("dp"), rows, rows, rows, rows, P("dp"), P("dp"), P("dp", "tensor"),
                   P(("tensor", "dp")), P("tensor", "dp"), P("dp")),
        check_vma=False,
    )
```

```python
import functools

import jax
import jax.numpy as jnp
from jax import lax
from jax.experimental import pallas as pl
from jax.experimental.pallas import tpu as pltpu
from jax.sharding import PartitionSpec as P

EPS = 1e-05
BLK = 256
PAIR = 128
HEAD = 64
C0 = 0.7978845608028654
C1 = 0.044715
F32 = jnp.float32
BF = jnp.bfloat16
VM = pltpu.VMEM


def nn(a, b):
    return lax.dot_general(a, b, (((1,), (0,)), ((), ())), preferred_element_type=F32)


def nt(a, b):
    return lax.dot_general(a, b, (((1,), (1,)), ((), ())), preferred_element_type=F32)


def tn(a, b):
    return lax.dot_general(a, b, (((0,), (0,)), ((), ())), preferred_element_type=F32)


def mean(v):
    return jnp.mean(v, axis=-1, keepdims=True)


def normed(v):
    centered = v - mean(v)
    scale = lax.rsqrt(mean(centered * centered) + EPS)
    return centered * scale, scale


def norm_back(e, hat, scale, gain):
    eg = e * gain
    return scale * (eg - mean(eg) - hat * mean(eg * hat))


def feature(v):
    return jnp.where(v > 0, v + 1.0, jnp.exp(jnp.minimum(v, 0.0)))


def ends_of(len_ref, n_images):
    ends, total = [], 0
    for i in range(n_images):
        total = total + len_ref[0, i]
        ends.append(total)
    return ends


def segment_of(places, ends):
    seg = jnp.zeros(places.shape, jnp.int32)
    for end in ends:
        seg = seg + jnp.where(places >= end, 1, 0)
    return seg


def scalar_segment(place, ends):
    seg = 0
    for end in ends:
        seg = seg + jnp.where(place >= end, 1, 0)
    return seg


def head_masks():
    lane = lax.broadcasted_iota(jnp.int32, (1, PAIR), 1)
    first = jnp.where(lane < HEAD, 1.0, 0.0).astype(BF)
    return first, (1.0 - first.astype(F32)).astype(BF)


def block_diagonal():
    row = lax.broadcasted_iota(jnp.int32, (PAIR, 2 * PAIR), 0)
    lane = lax.broadcasted_iota(jnp.int32, (PAIR, 2 * PAIR), 1)
    return jnp.where((row < HEAD) == (lax.rem(lane, PAIR) < HEAD), 1.0, 0.0)


def block_masks(b, ends):
    col = segment_of(b * BLK + lax.broadcasted_iota(jnp.int32, (BLK, 1), 0), ends)
    row = segment_of(b * BLK + lax.broadcasted_iota(jnp.int32, (1, BLK), 1), ends)
    before = jnp.where(b > 0, scalar_segment(b * BLK - 1, ends), -1)
    last = scalar_segment(b * BLK + BLK - 1, ends)
    t = lax.broadcasted_iota(jnp.int32, (BLK, BLK), 0)
    s = lax.broadcasted_iota(jnp.int32, (BLK, BLK), 1)
    same = col == row
    down = jnp.where(same & (t >= s), 1.0, 0.0).astype(BF)
    up = jnp.where(same & (t <= s), 1.0, 0.0).astype(BF)
    cont = jnp.where(col == before, 1.0, 0.0).astype(BF)
    trail = jnp.where(col == last, 1.0, 0.0).astype(BF)
    return down, up, cont, trail


def two(v):
    return jnp.concatenate([v, v], axis=0)


FIRST = (64,) * 4 + (128,) * 6
SECOND = (128,) * 7 + (64, 32, 32)
MESH_ID = pl.DeviceIdType.MESH
QUARTERS = 4


TICKS = {
    "F1b": [("mid", 0, 0)],
    "F1d": [("mid", 0, 1)],
    "F1e": [("mid", 0, 2)],
    "F2b": [("mid", 0, 3), ("tot", 0, 0), ("tot", 0, 1)],
    "F2d": [("mid", 0, 4), ("tot", 0, 2)],
    "F2e": [("tot", 0, 3)],
    "F3b": [("mid", 0, 5), ("tot", 0, 4)],
    "W0": [("mid", 0, 6)],
    "W1": [("tot", 0, 5)],
    "W3": [("mid", 0, 7)],
    "J1n": [("tot", 0, 6)],
    "J1a": [("start", 0), ("add", "down")],
    "J1p1": [("mid", 0, 8), ("add", "up")],
    "J1p3": [("start", 1), ("start", 2), ("tot", 0, 7)],
    "J1p5": [("start", 3)],
    "J1p7": [("mid", 0, 9)],
    "J1e": [("start", 4), ("tot", 0, 8)],
    "J2p1": [("mid", 1, 0), ("start", 5), ("start", 6), ("start", 7), ("start", 8)],
    "J2p3": [("second", "down"), ("tot", 0, 9)],
    "J2p7": [("last", "down"), ("mid", 1, 1)],
    "J2e": [("tot", 1, 0)],
    "N3": [("second", "up")],
    "O0": [("mid", 1, 2)],
    "O1": [("tot", 1, 1)],
    "G0a": [("last", "up"), ("add", "out")],
    "G0b": [("mid", 1, 3)],
    "G0c": [("start", 9), ("tot", 1, 2)],
    "G1a": [("add", 0)],
    "G1b": [("second", "out"), ("mid", 1, 4)],
    "G1c": [("tot", 1, 3)],
    "G2a": [("second", 0), ("mid", 1, 5), ("add", 1)],
    "G2b": [("last", "out"), ("tot", 1, 4)],
    "G2c": [("mid", 1, 6), ("add", 2)],
    "G3a": [("tot", 1, 5)],
    "G3b": [("last", 0), ("second", 1)],
    "G3c": [("second", 2), ("mid", 1, 7), ("mid", 1, 8), ("tot", 1, 6), ("add", 3)],
    "I2": [("tot", 1, 7)],
    "I3": [("second", 3), ("mid", 1, 9), ("tot", 1, 8), ("tot", 1, 9)],
    "END": [("last", 1), ("last", 2), ("last", 3)],
}


class Sums:
    def __init__(self, index, p, far, total, send, recv, sizes):
        z = lax.axis_index("tensor")
        self.sizes, self.starts = sizes, [sum(sizes[:i]) for i in range(len(sizes))]
        self.index, self.p, self.far, self.total, self.send, self.recv = index, p, far, total, send, recv
        self.middle = (z == 1) | (z == 2)
        self.end = (z == 0) | (z == 3)
        self.near = jnp.where(z == 0, 1, 2)
        self.mate = 3 - z
        self.edge = jnp.where(z == 1, 0, 3)

    def rows(self, c):
        return pl.ds(self.starts[c], self.sizes[c])

    def of_block(self, b):
        return [c for c in range(len(self.sizes)) if self.starts[c] // BLK == b]

    def copy(self, s, d, kind_s, kind_r, c, to):
        r = self.rows(c)
        return pltpu.make_async_remote_copy(
            src_ref=s.at[r, :], dst_ref=d.at[r, :], send_sem=self.send.at[self.index, kind_s, c],
            recv_sem=self.recv.at[self.index, kind_r, c], device_id={"tensor": to}, device_id_type=MESH_ID)

    def out(self, c):
        return self.copy(self.p, self.far, 0, 0, c, self.near)

    def across(self, c):
        return self.copy(self.p, self.total, 0, 1, c, self.mate)

    def back(self, c):
        return self.copy(self.total, self.total, 1, 1, c, self.edge)

    def start(self, c):
        pl.when(self.end)(lambda: self.out(c).start())

    def mid(self, c):
        @pl.when(self.middle)
        def _():
            r = self.rows(c)
            self.out(c).wait_recv()
            self.p[r, :] = self.p[r, :] + self.far[r, :]
            self.across(c).start()

    def tot(self, c, then=None):
        @pl.when(self.middle)
        def _():
            r = self.rows(c)
            self.across(c).wait_recv()
            self.total[r, :] = self.p[r, :] + self.total[r, :]
            self.back(c).start()
            if then is not None:
                then(c)

    def got(self, c, then=None):
        @pl.when(self.end)
        def _():
            self.back(c).wait_recv()
            if then is not None:
                then(c)

    def finish(self, c):
        pl.when(self.end)(lambda: self.out(c).wait_send())

        @pl.when(self.middle)
        def _():
            self.across(c).wait_send()
            self.back(c).wait_send()


class Scatter:
    def __init__(self, job, gw, rx, send, recv, credit, width):
        d = lax.axis_index("dp")
        self.half = width // 2
        self.job, self.gw, self.rx, self.send, self.recv, self.credit = job, gw, rx, send, recv, credit
        self.core, self.x, self.y = lax.rem(d, 2), lax.rem(d // 2, 2), d // 4
        self.by_core = self.y * 4 + self.x * 2 + (1 - self.core)
        self.by_x = self.y * 4 + (1 - self.x) * 2 + self.core
        self.by_y = (1 - self.y) * 4 + self.x * 2 + self.core

    def copy(self, stage, h, s, d, to):
        return pltpu.make_async_remote_copy(
            src_ref=s, dst_ref=d, send_sem=self.send.at[self.job, stage, h], recv_sem=self.recv.at[self.job, stage, h],
            device_id={"dp": to}, device_id_type=MESH_ID)

    def cols(self, h):
        return pl.ds(h * self.half, self.half)

    def c0(self, h):
        return self.copy(0, h, self.gw.at[:, :, 1 - self.core, :, self.cols(h)], self.rx.at[0:2, :, :, self.cols(h)], self.by_core)

    def c1(self, h):
        to = self.rx.at[2, :, :, self.cols(h)]
        if h == 0:
            return self.copy(1, h, self.gw.at[:, 1 - self.x, self.core, :, self.cols(h)], to, self.by_x)
        return self.copy(1, h, self.gw.at[1 - self.y, :, self.core, :, self.cols(h)], to, self.by_y)

    def c2(self, h):
        to = self.rx.at[3, 0, :, self.cols(h)]
        if h == 0:
            return self.copy(2, h, self.gw.at[1 - self.y, self.x, self.core, :, self.cols(h)], to, self.by_y)
        return self.copy(2, h, self.gw.at[self.y, 1 - self.x, self.core, :, self.cols(h)], to, self.by_x)

    def begin(self, h):
        self.c0(h).start()

    def add(self, h):
        self.c0(h).wait_recv()
        c = self.cols(h)
        for y in range(2):
            for x in range(2):
                self.gw[y, x, self.core, :, c] = self.gw[y, x, self.core, :, c] + self.rx[y, x, :, c]
        self.c1(h).start()

    def second(self, h):
        self.c1(h).wait_recv()
        c = self.cols(h)
        for i in range(2):
            y, x = (i, self.x) if h == 0 else (self.y, i)
            self.gw[y, x, self.core, :, c] = self.gw[y, x, self.core, :, c] + self.rx[2, i, :, c]
        self.c2(h).start()

    def last(self, h):
        self.c2(h).wait_recv()
        c = self.cols(h)
        return self.gw[self.y, self.x, self.core, :, c].astype(F32) + self.rx[3, 0, :, c].astype(F32)

    def sent(self):
        for h in range(2):
            self.c0(h).wait_send()
            self.c1(h).wait_send()
            self.c2(h).wait_send()

    def give(self):
        for to in (self.by_core, self.by_x, self.by_y):
            pl.semaphore_signal(self.credit, inc=1, device_id={"dp": to}, device_id_type=MESH_ID)

    def take(self):
        pl.semaphore_wait(self.credit, 3)


def layer_kernel(
    n_images, fused, dp,
    len_ref, g1, b1, g2, b2, bup, bd,
    x_h, cot_h, wq_h, wk_h, wv_h, wo_h, wu_h, wd_h,
    out_h, gi_h, gu_o, gd_o, go_o, gq_o, gk_o, gv_o, vec_o,
    x, cot, wq, wk, wv, wo, wu, wd,
    n1, pq, pk, va, rd, at, al, st, mid, n2, hid, gu, pn, pd, far, tot, tot2,
    gwb, rxa, rxb, ogd, vec, rv,
    in_sem, out_sem, og_sem, zs, zr, ss, sr, vs, vr, credit,
):
    width = cot.shape[1]
    blocks = cot.shape[0] // BLK
    tiles = width // BLK
    z = lax.axis_index("tensor")
    d = lax.axis_index("dp")
    loads = [(x_h.at[0, 0], x.at[0, 0]), (wq_h, wq), (wk_h, wk), (wv_h, wv), (x_h.at[0, 1], x.at[0, 1]), (x_h.at[1], x.at[1]),
             (wo_h, wo), (wu_h, wu), (cot_h, cot), (wd_h, wd)]
    loads = [pltpu.make_async_copy(s, t, in_sem.at[i]) for i, (s, t) in enumerate(loads)]
    for c in loads[:4]:
        c.start()
    first = Sums(0, pn, far, tot, zs, zr, FIRST)
    second = Sums(1, pd, n2, tot2, zs, zr, SECOND)
    barrier = pltpu.get_barrier_semaphore()
    if fused:
        for k in range(1, dp):
            pl.semaphore_signal(barrier, inc=1, device_id={"dp": lax.rem(d + k, dp)}, device_id_type=MESH_ID)

    @pl.when(first.end)
    def _():
        pl.semaphore_signal(barrier, inc=1, device_id={"tensor": first.near}, device_id_type=MESH_ID)

    @pl.when(first.middle)
    def _():
        pl.semaphore_signal(barrier, inc=1, device_id={"tensor": first.mate}, device_id_type=MESH_ID)
        pl.semaphore_signal(barrier, inc=1, device_id={"tensor": first.edge}, device_id_type=MESH_ID)

    ends = ends_of(len_ref, n_images)
    m0, m1 = head_masks()
    ones = jnp.ones((BLK, PAIR), BF)
    diagonal = block_diagonal()
    vec[...] = jnp.zeros_like(vec)
    once = jnp.where(z == 1, 1.0, 0.0)
    matrix = lambda ref: ref[...].reshape(width, width)
    apart = pl.when(z >= 0)

    def at_step(j, k, *acts):
        @pl.when(j == k)
        def _():
            for act in acts:
                act()

    def act(kind, which, *more):
        if kind == "add":
            add(which)
        elif kind == "second":
            stage(which)
        elif kind == "last":
            last(which)
        elif kind == "start":
            second.start(which)
        elif kind == "mid":
            (first, second)[which].mid(*more)
        elif which == 0:
            first.tot(*more)
        else:
            second.tot(*more, emit)

    def tick(place, at=None):
        acts = [functools.partial(act, *a) for a in TICKS.get(place, ())]
        if at is None:
            for a in acts:
                a()
        elif acts:
            at_step(*at, *acts)

    def forward_block(b, _):
        rows = pl.ds(pl.multiple_of(b * BLK, BLK), BLK)
        at_step(b, 0, loads[0].wait)
        xb = x[b // 2, lax.rem(b, 2)].reshape(BLK, width).astype(F32)
        hat, _ = normed(xb)
        n1b = (hat * g1[...] + b1[...]).astype(BF)
        n1[:, rows] = n1b.T
        at_step(b, 0, loads[1].wait, loads[6].start, loads[7].start)
        pq[rows, :] = feature(nn(n1b, wq[...]).astype(BF).astype(F32)).astype(BF)
        at_step(b, 0, loads[2].wait, loads[8].start, loads[9].start, loads[4].start, loads[5].start)
        pk[rows, :] = feature(nn(n1b, wk[...]).astype(BF).astype(F32)).astype(BF)
        at_step(b, 0, loads[3].wait)
        va[rows, :] = nn(n1b, wv[...]).astype(BF)
        down, _, cont, trail = block_masks(b, ends)
        down2 = two(down)
        for p in range(width // PAIR):
            lanes = slice(p * PAIR, (p + 1) * PAIR)
            q, k, v = pq[rows, lanes], pk[rows, lanes], va[rows, lanes]
            a = nt(jnp.concatenate([q * m0, q * m1], axis=0), k).astype(BF) * down2
            o = nn(a[:BLK], jnp.concatenate([v * m0, ones * m0], axis=1))
            o = o + nn(a[BLK:], jnp.concatenate([v * m1, ones * m1], axis=1))
            before = jnp.where(b > 0, st[jnp.maximum(b - 1, 0), p].astype(F32), 0.0).astype(BF)
            o = o + nn(q * cont, before)
            st[b, p] = (tn(k * trail, jnp.concatenate([v, ones], axis=1)) * diagonal).astype(BF)
            inverse = 1.0 / o[:, PAIR:]
            rd[rows, lanes] = inverse.astype(BF)
            attended = o[:, :PAIR] * inverse
            attended_low = attended.astype(BF)
            at[rows, lanes] = attended_low
            al[rows, lanes] = (attended - attended_low.astype(F32)).astype(BF)

        @pl.when(b == 0)
        def _():
            count = (dp - 1) if fused else 0
            pl.when(first.end)(lambda: pl.semaphore_wait(barrier, count + 1))
            pl.when(first.middle)(lambda: pl.semaphore_wait(barrier, count + 2))
            for i in range(4, 8):
                loads[i].wait()

        for k in range(1, blocks):
            tick(f"F{k}b", (b, k))
        middle = xb + nn(at[rows, :], wo[...])
        mid[rows, :] = middle
        hat2, _ = normed(middle)
        n2b = (hat2 * g2[...] + b2[...]).astype(BF)
        n2[:, rows] = n2b.T
        at_step(b, 0, loads[8].wait, loads[9].wait)
        cb = cot[rows, :]
        vec[0:1, :] += jnp.sum(cb.astype(F32), axis=0, keepdims=True)
        for c in range(tiles):
            cols = slice(c * BLK, (c + 1) * BLK)
            u = nn(n2b, wu[..., cols].reshape(width, BLK)) + bup[:, cols]
            gh = nt(cb, wd[c].reshape(BLK, width))
            th = jnp.tanh(C0 * (u + C1 * u * u * u))
            hid[rows, cols] = (0.5 * u * (1.0 + th)).astype(BF)
            slope = 0.5 * (1.0 + th) + 0.5 * u * (1.0 - th * th) * (C0 * (1.0 + 3.0 * C1 * u * u))
            gub = (gh * slope).astype(BF)
            gu[rows, cols] = gub
            vec[1:2, cols] += jnp.sum(gub.astype(F32), axis=0, keepdims=True)
        for k in range(1, blocks):
            tick(f"F{k}d", (b, k))
        pn[rows, :] = nt(gu[rows, :], matrix(wu)).astype(BF)
        for k in range(blocks):
            at_step(b, k, *[functools.partial(first.start, c) for c in first.of_block(k)])
        pd[rows, :] = (nn(hid[rows, :], matrix(wd)) + once * (middle + bd[...])).astype(BF)
        for k in range(1, blocks):
            tick(f"F{k}e", (b, k))
        return 0

    lax.fori_loop(0, blocks, forward_block, 0)

    groups = tiles
    jobs = {}
    slots = ((x, rxa), (gwb, rxb), (wu, wd))
    for i, name in enumerate(["up", "down", "out"] + list(range(groups))):
        gw, rx = slots[i % 3]
        jobs[name] = Scatter(i, gw, rx, ss, sr, credit.at[i % 3], 3 * BLK if i > 2 else width)
    last_job = 2 + groups

    def put(name, col, value):
        gw = jobs[name].gw
        gw[..., col:col + value.shape[1]] = value.astype(BF).reshape(gw.shape[:-1] + (value.shape[1],))

    def send_whole(name, targets):
        gw = jobs[name].gw
        copies = []
        for y in range(2):
            for x_ in range(2):
                for k in range(2):
                    row = pl.ds((y * 4 + x_ * 2 + k) * (width // 8), width // 8)
                    for n, (o, col, o_col, wide) in enumerate(targets):
                        copies.append(pltpu.make_async_copy(gw.at[y, x_, k, :, col:col + wide], o.at[row, o_col:o_col + wide],
                                                            og_sem.at[0]))
        for c in copies:
            c.start()
            c.wait()

    def gradient(name, l, r, half):
        wide = width // 2
        for c in range(half * wide, (half + 1) * wide, BLK):
            apart(lambda: put(name, c, nn(l[...], r[:, c:c + BLK])))
        if fused:
            jobs[name].begin(half)
        elif half == 1:
            send_whole(name, [({"up": gu_o, "down": gd_o, "out": go_o}[name], 0, 0, width)])

    def projections(g):
        cols = slice(g * BLK, (g + 1) * BLK)
        apart(lambda: put(g, 0, nn(n1[...], rd[:, cols])))
        apart(lambda: put(g, BLK, nn(n1[...], al[:, cols])))
        if fused:
            jobs[g].begin(0)
        apart(lambda: put(g, 2 * BLK, nn(n1[...], va[:, cols])))
        if fused:
            jobs[g].begin(1)
        else:
            send_whole(g, [(o, i * BLK, g * BLK, BLK) for i, o in enumerate((gq_o, gk_o, gv_o))])

    def turn(ref):
        def part(c, _):
            rows = pl.ds(pl.multiple_of(c * BLK, BLK), BLK)
            gu[:, rows] = ref[rows, :].T
            return 0

        lax.fori_loop(0, blocks, part, 0)

    def ready(name):
        if fused:
            jobs[name].take()
            for c in out_copies({"out": None, 0: "up", 1: "down", 2: "out", 3: 0}[name]) if name != "out" else ():
                c.wait()

    def add(name):
        if fused:
            for h in range(2):
                jobs[name].add(h)

    def stage(name):
        if fused:
            for h in range(2):
                jobs[name].second(h)

    def out_copies(name):
        if name == "down":
            return [pltpu.make_async_copy(ogd, gd_o, og_sem.at[1])]
        s = jobs[name]
        mine = s.gw.at[s.y, s.x, s.core]
        if name in ("up", "out"):
            return [pltpu.make_async_copy(mine, gu_o if name == "up" else go_o, og_sem.at[s.job])]
        return [pltpu.make_async_copy(mine.at[:, i * BLK:(i + 1) * BLK], o.at[:, name * BLK:(name + 1) * BLK],
                                      og_sem.at[3 + 3 * name + i]) for i, o in enumerate((gq_o, gk_o, gv_o))]

    def last(name):
        if not fused:
            return
        s = jobs[name]
        for h in range(2):
            v = s.last(h)
            if name == "down":
                ogd[h * s.half:(h + 1) * s.half, :] = v.T.astype(BF)
            else:
                s.gw[s.y, s.x, s.core, :, s.cols(h)] = v.astype(BF)
        for c in out_copies(name):
            c.start()
        s.sent()
        if s.job + 3 <= last_job:
            s.give()

    if fused:
        jobs["out"].give()
    gradient("up", n2, gu, 0)
    tick("W0")
    gradient("up", n2, gu, 1)
    tick("W1")
    turn(cot)
    gradient("down", gu, hid, 0)
    tick("W2")
    gradient("down", gu, hid, 1)
    tick("W3")

    def reload(b, k):
        return pltpu.make_async_copy(x_h.at[b // 2, lax.rem(b, 2), k],
                                     hid.at[pl.ds(pl.multiple_of(b * BLK + k * PAIR, PAIR), PAIR), :], in_sem.at[2 * b + k])

    for b in range(blocks):
        for k in range(2):
            reload(b, k).start()

    row = lax.broadcasted_iota(jnp.int32, (2 * PAIR, 2 * PAIR), 0) // HEAD
    lane = lax.broadcasted_iota(jnp.int32, (2 * PAIR, 2 * PAIR), 1) // HEAD
    same_head = jnp.where(row == lane, 1.0, 0.0).astype(BF)
    half_lane = lax.rem(lax.broadcasted_iota(jnp.int32, (1, BLK), 1), HEAD) < HEAD // 2

    def norm_block(b):
        rows = pl.ds(pl.multiple_of(b * BLK, BLK), BLK)
        for k in range(blocks):
            if isinstance(b, int):
                for c in first.of_block(k) if k == b else ():
                    first.got(c)
            else:
                at_step(b, k, *[functools.partial(first.got, c) for c in first.of_block(k)])
        hat, scale = normed(mid[rows, :])
        e = tot[rows, :].astype(F32)
        vec[2:3, :] += jnp.sum(e * hat, axis=0, keepdims=True)
        vec[3:4, :] += jnp.sum(e, axis=0, keepdims=True)
        gm = cot[rows, :].astype(F32) + norm_back(e, hat, scale, g2[...])
        mid[rows, :] = gm
        gbb = gm.astype(BF)
        cot[rows, :] = gbb
        ga = nt(gbb, wo[...])
        n = (ga * rd[rows, :].astype(F32)).astype(BF)
        prod = n.astype(F32) * (at[rows, :].astype(F32) + al[rows, :].astype(F32))
        rd[rows, :] = n
        high = prod.astype(BF)
        rest = (prod - high.astype(F32)).astype(BF)
        for c in range(tiles):
            cols = slice(c * BLK, (c + 1) * BLK)
            m = (nn(high[:, cols], same_head) + nn(rest[:, cols], same_head)) * (-2.0 / HEAD)
            m_high = m.astype(BF).astype(F32)
            al[rows, cols] = jnp.where(half_lane, m_high, m - m_high).astype(BF)

    emit = lambda c: pltpu.make_async_copy(tot2.at[second.rows(c), :], out_h.at[second.rows(c), :], out_sem.at[0, c]).start()

    def core_masks(b):
        after_b = jnp.minimum(b + 1, blocks - 1)
        low, up, cont, trail = block_masks(b, ends)
        more = jnp.where(b < blocks - 1, 1.0, 0.0)
        cont_after = (block_masks(after_b, ends)[2].astype(F32) * more).astype(BF)
        return two(low), two(up), cont, trail, cont_after

    def core_pair(b, p, masks):
        low2, up2, cont, trail, cont_after = masks
        rows = pl.ds(pl.multiple_of(b * BLK, BLK), BLK)
        after_rows = pl.ds(pl.multiple_of(jnp.minimum(b + 1, blocks - 1) * BLK, BLK), BLK)
        lanes = slice(p * PAIR, (p + 1) * PAIR)
        q, k, v = pq[rows, lanes], pk[rows, lanes], va[rows, lanes]
        n, m = rd[rows, lanes], al[rows, lanes]
        nm_after = jnp.concatenate([rd[after_rows, lanes], al[after_rows, lanes]], axis=1)
        after = (tn(pq[after_rows, lanes] * cont_after, nm_after) * diagonal).astype(BF)
        q0, q1, k0, k1, n0, n1_ = q * m0, q * m1, k * m0, k * m1, n * m0, n * m1
        nm = jnp.concatenate([n, m], axis=1)
        nm2 = jnp.concatenate(
            [jnp.concatenate([n0, m * m0], axis=1), jnp.concatenate([n1_, m * m1], axis=1)], axis=0
        )
        v1 = jnp.concatenate([v, ones], axis=1)
        v2 = jnp.concatenate(
            [jnp.concatenate([v * m0, ones * m0], axis=1), jnp.concatenate([v * m1, ones * m1], axis=1)], axis=0
        )
        da = nt(nm2, v1).astype(BF) * low2
        dat = nt(v2, nm).astype(BF) * up2
        a_t = nt(jnp.concatenate([k0, k1], axis=0), q).astype(BF) * up2
        before = jnp.where(b > 0, st[jnp.maximum(b - 1, 0), p].astype(F32), 0.0).astype(BF)
        dq = nn(da[:BLK], k0) + nn(da[BLK:], k1) + nt(nm * cont, before)
        dk = nn(dat[:BLK], q0) + nn(dat[BLK:], q1) + nt(v1 * trail, after)
        dv = nn(a_t[:BLK], n0) + nn(a_t[BLK:], n1_) + nn(k * trail, after[:, :PAIR])
        rd[rows, lanes] = (dq * jnp.minimum(q.astype(F32), 1.0)).astype(BF)
        al[rows, lanes] = (dk * jnp.minimum(k.astype(F32), 1.0)).astype(BF)
        va[rows, lanes] = dv.astype(BF)

    def input_block(b):
        rows = pl.ds(pl.multiple_of(b * BLK, BLK), BLK)
        e = nt(rd[rows, :], wq[...]) + nt(al[rows, :], wk[...]) + nt(va[rows, :], wv[...])
        for k in range(2):
            reload(b, k).wait()
        hat, scale = normed(hid[rows, :].astype(F32))
        vec[4:5, :] += jnp.sum(e * hat, axis=0, keepdims=True)
        vec[5:6, :] += jnp.sum(e, axis=0, keepdims=True)
        hid[rows, :] = (mid[rows, :] + norm_back(e, hat, scale, g1[...])).astype(BF)
        pltpu.make_async_copy(hid.at[rows, :], gi_h.at[rows, :], out_sem.at[1, b]).start()

    def backward_step(j, _):
        for k in range(blocks - 1):
            tick(f"J{k}n", (j, k))
        apart(lambda: norm_block(j))
        for k in range(blocks - 1):
            tick(f"J{k}a", (j, k))

        @pl.when(j > 0)
        def _():
            masks = core_masks(j - 1)
            for p in range(width // PAIR):
                core_pair(j - 1, p, masks)
                for k in range(1, blocks - 1):
                    tick(f"J{k}p{p}", (j, k))
            apart(lambda: input_block(j - 1))

        for k in range(1, blocks - 1):
            tick(f"J{k}e", (j, k))
        return 0

    lax.fori_loop(0, blocks - 1, backward_step, 0)
    apart(lambda: norm_block(blocks - 1))
    tick("N3")
    ready("out")
    turn(at)
    gradient("out", gu, cot, 0)
    tick("O0")
    gradient("out", gu, cot, 1)
    tick("O1")

    def late_group(b, g):
        masks = core_masks(b)
        for p in (2 * g, 2 * g + 1):
            core_pair(b, p, masks)

    for g in range(groups):
        apart(functools.partial(late_group, blocks - 2, g))
        tick(f"G{g}a")
        apart(functools.partial(late_group, blocks - 1, g))
        tick(f"G{g}b")
        ready(g)
        projections(g)
        tick(f"G{g}c")
    apart(lambda: input_block(blocks - 2))
    tick("I2")
    apart(lambda: input_block(blocks - 1))
    tick("I3")
    if fused:
        own = pl.ds(pl.multiple_of(d * (width // dp), width // dp), width // dp)
        small = []
        for k in range(1, dp):
            to = lax.rem(d + k, dp)
            cols = pl.ds(pl.multiple_of(to * (width // dp), width // dp), width // dp)
            small.append(pltpu.make_async_remote_copy(
                src_ref=vec.at[:, cols], dst_ref=rv.at[k], send_sem=vs.at[k], recv_sem=vr.at[k],
                device_id={"dp": to}, device_id_type=MESH_ID))
        for c in small:
            c.start()
    tick("END")
    if fused:
        total = vec[:, own]
        for c in small:
            c.wait_recv()
        for k in range(1, dp):
            total = total + rv[k]
        vec_o[...] = total
        for c in small:
            c.wait_send()
    else:
        vec_o[...] = vec[...]
    for c in range(len(SECOND)):
        second.got(c, emit)
    for c in range(len(FIRST)):
        first.finish(c)
    for c in range(len(SECOND)):
        second.finish(c)
        pltpu.make_async_copy(tot2.at[second.rows(c), :], out_h.at[second.rows(c), :], out_sem.at[0, c]).wait()
    for b in range(blocks):
        rows = pl.ds(b * BLK, BLK)
        pltpu.make_async_copy(hid.at[rows, :], gi_h.at[rows, :], out_sem.at[1, b]).wait()
    if fused:
        for name in (1, 2, 3):
            for c in out_copies(name):
                c.wait()


def finish_kernel(out_h, gi_h, *refs):
    weights, vec = refs[:6], refs[6]
    out_o, gi_o = refs[7:9]
    weights_o, vecs_o = refs[9:15], refs[15:21]
    narrow, wide, small, small_wide, tall, tall_wide, passed, sem_in, sem_out, sem = refs[21:]
    rows = gi_h.shape[0] // 8
    part = lambda c: pl.ds(c * rows, rows)
    ins = [pltpu.make_async_copy(gi_h.at[part(c), :], narrow.at[part(c), :], sem_in.at[c]) for c in range(8)]
    outs = [pltpu.make_async_copy(wide.at[part(c), :], gi_o.at[part(c), :], sem_out.at[c]) for c in range(8)]
    where = [(tall, tall_wide) if i == 1 else (small.at[i], small_wide.at[i]) for i in range(6)]
    ins += [pltpu.make_async_copy(weights[i], where[i][0], sem_in.at[8 + i]) for i in range(6)]
    outs += [pltpu.make_async_copy(where[i][1], weights_o[i], sem_out.at[8 + i]) for i in range(6)]
    for c in ins[:8]:
        c.start()
    for c in ins[8:]:
        c.start()
    through = [[pltpu.make_async_copy(s.at[part(c), :], t.at[part(c), :], sem.at[i, c])
                for i, (s, t) in enumerate(((out_h, passed), (passed, out_o)))] for c in range(8)]
    for c in through:
        c[0].start()
    for i, o in enumerate(vecs_o):
        o[...] = vec[i, :]
    for c in range(8):
        ins[c].wait()
        wide[part(c), :] = narrow[part(c), :].astype(F32)
        outs[c].start()
    for i in range(6):
        ins[8 + i].wait()
        where[i][1][...] = where[i][0][...].astype(F32)
        outs[8 + i].start()
    for c in through:
        c[0].wait()
        c[1].start()
    for c in outs:
        c.wait()
    for c in through:
        c[1].wait()


def per_device(dp, inputs, cotangent, lengths, ln1_gain, ln1_bias, w_query, w_key, w_value, w_out, ln2_gain, ln2_bias, w_up, b_up,
               w_down, b_down):
    tokens, width = inputs.shape
    n_images = lengths.shape[1]
    fused = dp == 8
    blocks, pairs = tokens // BLK, width // PAIR
    shape = jax.ShapeDtypeStruct
    full = shape((tokens, width), BF)
    piece, square = shape((width // dp, width), BF), shape((width, width), BF)
    tall = shape((width, width // dp), BF)
    anyspace = pl.BlockSpec(memory_space=pl.ANY)
    vmem = pl.BlockSpec(memory_space=VM)
    smem = pl.BlockSpec(memory_space=pltpu.SMEM)
    row = lambda v: v.reshape(1, -1)
    big = lambda dtype=BF: VM((tokens, width), dtype)
    weight = VM((width, width), BF)
    split = (2, 2, 2, width // 8, width)
    boxed = VM(split, BF)
    received = VM((4, 2, width // 8, width), BF)
    dma = pltpu.SemaphoreType.DMA
    weights_out = [piece, tall] + [piece] * 4 if fused else [square] * 6
    pieces = max(len(FIRST), len(SECOND))
    outs = pl.pallas_call(
        functools.partial(layer_kernel, n_images, fused, dp),
        out_shape=[full, full] + weights_out + [shape((8, width // dp if fused else width), F32)],
        in_specs=[smem] + [vmem] * 6 + [anyspace] * 8,
        out_specs=[anyspace] * 8 + [vmem],
        scratch_shapes=[boxed, big()] + [weight] * 4 + [boxed, received] + [big()] * 7
        + [VM((blocks, pairs, PAIR, 2 * PAIR), BF), big(F32)] + [big()] * 8
        + [boxed, received, received, VM((width, width // 8), BF), VM((8, width), F32),
           VM((8, 8, width // 8), F32)]
        + [dma((10,)), dma((2, pieces)), dma((15,)), dma((2, 2, pieces)), dma((2, 2, pieces)), dma((7, 3, 2)), dma((7, 3, 2)),
           dma((8,)), dma((8,)), pltpu.SemaphoreType.REGULAR((3,))],
        compiler_params=pltpu.CompilerParams(vmem_limit_bytes=VMEM_LIMIT, collective_id=0, has_side_effects=True),
    )(lengths, row(ln1_gain), row(ln1_bias), row(ln2_gain), row(ln2_bias), row(b_up), row(b_down),
      inputs.reshape(split), cotangent, w_query, w_key, w_value, w_out, w_up.reshape(split), w_down.reshape(4, 2, width // 8, width))
    out, gi, gu, gd, go, gq, gk, gv, vec = outs
    if fused:
        wide = lambda s: shape(s.shape, F32)
        small = shape((width // dp,), F32)
        outs = pl.pallas_call(
            finish_kernel,
            out_shape=[full, wide(full)] + [wide(s) for s in weights_out] + [small] * 6,
            in_specs=[anyspace] * 8 + [vmem],
            out_specs=[anyspace] * 8 + [vmem] * 6,
            scratch_shapes=[big(), big(F32), VM((6,) + piece.shape, BF), VM((6,) + piece.shape, F32), VM(tall.shape, BF),
                            VM(tall.shape, F32), big(), dma((14,)), dma((14,)), dma((2, 8))],
            compiler_params=pltpu.CompilerParams(vmem_limit_bytes=VMEM_LIMIT),
        )(out, gi, gu, gd, go, gq, gk, gv, vec)
        out, gi, gu, gd, go, gq, gk, gv = outs[:8]
        vec = outs[8:]
    else:
        scatter = lambda v, axis=0: lax.psum_scatter(v, "dp", scatter_dimension=axis, tiled=True)
        gu, go, gq, gk, gv = (scatter(v).astype(F32) for v in (gu, go, gq, gk, gv))
        gd = scatter(gd).astype(F32).T
        vec = scatter(vec, 1)
        gi = gi.astype(F32)
    return (out, gi, vec[4], vec[5], gq, gk, gv, go, vec[2], vec[3], gu, vec[1], gd, vec[0])


VMEM_LIMIT = 64 << 20


def solution(mesh):
    rows, whole = P("dp", None), P()
    placed = (rows, rows, rows) + (whole,) * 8 + (P(None, "tensor"), P("tensor"), P("tensor", None), whole)
    return jax.shard_map(
        functools.partial(per_device, mesh.shape["dp"]),
        mesh=mesh,
        in_specs=placed,
        out_specs=(rows, rows, P("dp"), P("dp"), rows, rows, rows, rows, P("dp"), P("dp"), P("dp", "tensor"),
                   P(("tensor", "dp")), P("tensor", "dp"), P("dp")),
        check_vma=False,
    )
```

```python
import functools

import jax
import jax.numpy as jnp
from jax import lax
from jax.experimental import pallas as pl
from jax.experimental.pallas import tpu as pltpu
from jax.sharding import PartitionSpec as P

EPS = 1e-05
BLK = 256
PAIR = 128
HEAD = 64
C0 = 0.7978845608028654
C1 = 0.044715
F32 = jnp.float32
BF = jnp.bfloat16
VM = pltpu.VMEM


def nn(a, b):
    return lax.dot_general(a, b, (((1,), (0,)), ((), ())), preferred_element_type=F32)


def nt(a, b):
    return lax.dot_general(a, b, (((1,), (1,)), ((), ())), preferred_element_type=F32)


def tn(a, b):
    return lax.dot_general(a, b, (((0,), (0,)), ((), ())), preferred_element_type=F32)


def mean(v):
    return jnp.mean(v, axis=-1, keepdims=True)


def normed(v):
    centered = v - mean(v)
    scale = lax.rsqrt(mean(centered * centered) + EPS)
    return centered * scale, scale


def norm_back(e, hat, scale, gain):
    eg = e * gain
    return scale * (eg - mean(eg) - hat * mean(eg * hat))


def feature(v):
    return jnp.where(v > 0, v + 1.0, jnp.exp(jnp.minimum(v, 0.0)))


def ends_of(len_ref, n_images):
    ends, total = [], 0
    for i in range(n_images):
        total = total + len_ref[0, i]
        ends.append(total)
    return ends


def segment_of(places, ends):
    seg = jnp.zeros(places.shape, jnp.int32)
    for end in ends:
        seg = seg + jnp.where(places >= end, 1, 0)
    return seg


def scalar_segment(place, ends):
    seg = 0
    for end in ends:
        seg = seg + jnp.where(place >= end, 1, 0)
    return seg


def head_masks():
    lane = lax.broadcasted_iota(jnp.int32, (1, PAIR), 1)
    first = jnp.where(lane < HEAD, 1.0, 0.0).astype(BF)
    return first, (1.0 - first.astype(F32)).astype(BF)


def block_diagonal():
    row = lax.broadcasted_iota(jnp.int32, (PAIR, 2 * PAIR), 0)
    lane = lax.broadcasted_iota(jnp.int32, (PAIR, 2 * PAIR), 1)
    return jnp.where((row < HEAD) == (lax.rem(lane, PAIR) < HEAD), 1.0, 0.0)


def block_masks(b, ends):
    col = segment_of(b * BLK + lax.broadcasted_iota(jnp.int32, (BLK, 1), 0), ends)
    row = segment_of(b * BLK + lax.broadcasted_iota(jnp.int32, (1, BLK), 1), ends)
    before = jnp.where(b > 0, scalar_segment(b * BLK - 1, ends), -1)
    last = scalar_segment(b * BLK + BLK - 1, ends)
    t = lax.broadcasted_iota(jnp.int32, (BLK, BLK), 0)
    s = lax.broadcasted_iota(jnp.int32, (BLK, BLK), 1)
    same = col == row
    down = jnp.where(same & (t >= s), 1.0, 0.0).astype(BF)
    up = jnp.where(same & (t <= s), 1.0, 0.0).astype(BF)
    cont = jnp.where(col == before, 1.0, 0.0).astype(BF)
    trail = jnp.where(col == last, 1.0, 0.0).astype(BF)
    return down, up, cont, trail


def two(v):
    return jnp.concatenate([v, v], axis=0)


FIRST = (64,) * 4 + (128,) * 6
SECOND = (128,) * 7 + (64, 32, 32)
MESH_ID = pl.DeviceIdType.MESH
QUARTERS = 4


TICKS = {
    "F1b": [("mid", 0, 0)],
    "F1e": [("mid", 0, 1), ("mid", 0, 2)],
    "F2b": [("mid", 0, 3), ("tot", 0, 0)],
    "F2d": [("tot", 0, 1), ("tot", 0, 2)],
    "F2e": [("mid", 0, 4)],
    "F3b": [("mid", 0, 5), ("tot", 0, 3)],
    "F3d": [("tot", 0, 4)],
    "W0": [("mid", 0, 6)],
    "W1": [("tot", 0, 5)],
    "W3": [("mid", 0, 7)],
    "J0a": [("tot", 0, 6)],
    "J1n": [("add", "down"), ("add", "up")],
    "J1a": [("start", 0), ("mid", 0, 8)],
    "J1p3": [("tot", 0, 7)],
    "J1p7": [("mid", 0, 9), ("start", 1)],
    "J1e": [("start", 2), ("start", 3), ("tot", 0, 8)],
    "J2n": [("start", 4)],
    "J2a": [("second", "down")],
    "J2p1": [("second", "up"), ("mid", 1, 0), ("start", 5)],
    "J2p3": [("tot", 0, 9)],
    "J2p7": [("mid", 1, 1)],
    "J2e": [("last", "up"), ("start", 6), ("tot", 1, 0)],
    "O0": [("mid", 1, 2)],
    "O1": [("tot", 1, 1)],
    "G0b": [("mid", 1, 3), ("add", "out")],
    "G0c": [("last", "down"), ("tot", 1, 2)],
    "G1a": [("start", 7)],
    "G1b": [("mid", 1, 4), ("start", 8), ("add", 0)],
    "G1c": [("tot", 1, 3)],
    "G2a": [("second", "out"), ("mid", 1, 5), ("tot", 1, 4), ("add", 1)],
    "G2b": [("last", "out"), ("second", 0), ("mid", 1, 6), ("start", 9)],
    "G2c": [("tot", 1, 5)],
    "G3a": [("second", 1)],
    "G3b": [("last", 0), ("mid", 1, 7), ("mid", 1, 8), ("add", 2)],
    "G3c": [("tot", 1, 6), ("add", 3)],
    "I2": [("last", 1), ("second", 2), ("mid", 1, 9), ("tot", 1, 7), ("tot", 1, 8)],
    "I3": [("second", 3), ("tot", 1, 9)],
    "END": [("last", 2), ("last", 3)],
}


class Sums:
    def __init__(self, index, p, far, total, send, recv, sizes):
        z = lax.axis_index("tensor")
        self.sizes, self.starts = sizes, [sum(sizes[:i]) for i in range(len(sizes))]
        self.index, self.p, self.far, self.total, self.send, self.recv = index, p, far, total, send, recv
        self.middle = (z == 1) | (z == 2)
        self.end = (z == 0) | (z == 3)
        self.near = jnp.where(z == 0, 1, 2)
        self.mate = 3 - z
        self.edge = jnp.where(z == 1, 0, 3)

    def rows(self, c):
        return pl.ds(self.starts[c], self.sizes[c])

    def of_block(self, b):
        return [c for c in range(len(self.sizes)) if self.starts[c] // BLK == b]

    def copy(self, s, d, kind_s, kind_r, c, to):
        r = self.rows(c)
        return pltpu.make_async_remote_copy(
            src_ref=s.at[r, :], dst_ref=d.at[r, :], send_sem=self.send.at[self.index, kind_s, c],
            recv_sem=self.recv.at[self.index, kind_r, c], device_id={"tensor": to}, device_id_type=MESH_ID)

    def out(self, c):
        return self.copy(self.p, self.far, 0, 0, c, self.near)

    def across(self, c):
        return self.copy(self.p, self.total, 0, 1, c, self.mate)

    def back(self, c):
        return self.copy(self.total, self.total, 1, 1, c, self.edge)

    def start(self, c):
        pl.when(self.end)(lambda: self.out(c).start())

    def mid(self, c):
        @pl.when(self.middle)
        def _():
            r = self.rows(c)
            self.out(c).wait_recv()
            self.p[r, :] = self.p[r, :] + self.far[r, :]
            self.across(c).start()

    def tot(self, c, then=None):
        @pl.when(self.middle)
        def _():
            r = self.rows(c)
            self.across(c).wait_recv()
            self.total[r, :] = self.p[r, :] + self.total[r, :]
            self.back(c).start()
            if then is not None:
                then(c)

    def got(self, c, then=None):
        @pl.when(self.end)
        def _():
            self.back(c).wait_recv()
            if then is not None:
                then(c)

    def finish(self, c):
        pl.when(self.end)(lambda: self.out(c).wait_send())

        @pl.when(self.middle)
        def _():
            self.across(c).wait_send()
            self.back(c).wait_send()


class Scatter:
    def __init__(self, job, gw, rx, send, recv, credit, width):
        d = lax.axis_index("dp")
        self.half = width // 2
        self.job, self.gw, self.rx, self.send, self.recv, self.credit = job, gw, rx, send, recv, credit
        self.core, self.x, self.y = lax.rem(d, 2), lax.rem(d // 2, 2), d // 4
        self.by_core = self.y * 4 + self.x * 2 + (1 - self.core)
        self.by_x = self.y * 4 + (1 - self.x) * 2 + self.core
        self.by_y = (1 - self.y) * 4 + self.x * 2 + self.core

    def copy(self, stage, h, s, d, to):
        return pltpu.make_async_remote_copy(
            src_ref=s, dst_ref=d, send_sem=self.send.at[self.job, stage, h], recv_sem=self.recv.at[self.job, stage, h],
            device_id={"dp": to}, device_id_type=MESH_ID)

    def cols(self, h):
        return pl.ds(h * self.half, self.half)

    def c0(self, h):
        return self.copy(0, h, self.gw.at[:, :, 1 - self.core, :, self.cols(h)], self.rx.at[0:2, :, :, self.cols(h)], self.by_core)

    def c1(self, h):
        to = self.rx.at[2, :, :, self.cols(h)]
        if h == 0:
            return self.copy(1, h, self.gw.at[:, 1 - self.x, self.core, :, self.cols(h)], to, self.by_x)
        return self.copy(1, h, self.gw.at[1 - self.y, :, self.core, :, self.cols(h)], to, self.by_y)

    def c2(self, h):
        to = self.rx.at[3, 0, :, self.cols(h)]
        if h == 0:
            return self.copy(2, h, self.gw.at[1 - self.y, self.x, self.core, :, self.cols(h)], to, self.by_y)
        return self.copy(2, h, self.gw.at[self.y, 1 - self.x, self.core, :, self.cols(h)], to, self.by_x)

    def begin(self, h):
        self.c0(h).start()

    def add(self, h):
        self.c0(h).wait_recv()
        c = self.cols(h)
        for y in range(2):
            for x in range(2):
                self.gw[y, x, self.core, :, c] = self.gw[y, x, self.core, :, c] + self.rx[y, x, :, c]
        self.c1(h).start()

    def second(self, h):
        self.c1(h).wait_recv()
        c = self.cols(h)
        for i in range(2):
            y, x = (i, self.x) if h == 0 else (self.y, i)
            self.gw[y, x, self.core, :, c] = self.gw[y, x, self.core, :, c] + self.rx[2, i, :, c]
        self.c2(h).start()

    def last(self, h):
        self.c2(h).wait_recv()
        c = self.cols(h)
        return self.gw[self.y, self.x, self.core, :, c].astype(F32) + self.rx[3, 0, :, c].astype(F32)

    def sent(self):
        for h in range(2):
            self.c0(h).wait_send()
            self.c1(h).wait_send()
            self.c2(h).wait_send()

    def give(self):
        for to in (self.by_core, self.by_x, self.by_y):
            pl.semaphore_signal(self.credit, inc=1, device_id={"dp": to}, device_id_type=MESH_ID)

    def take(self):
        pl.semaphore_wait(self.credit, 3)


def layer_kernel(
    n_images, fused, dp,
    len_ref, g1, b1, g2, b2, bup, bd,
    x_h, cot_h, wq_h, wk_h, wv_h, wo_h, wu_h, wd_h,
    out_h, gi_h, gu_o, gd_o, go_o, gq_o, gk_o, gv_o, vec_o,
    x, cot, wq, wk, wv, wo, wu, wd,
    n1, pq, pk, va, rd, at, al, st, mid, n2, hid, gu, pn, pd, far, tot, tot2,
    gwb, rxa, rxb, ogd, vec, rv,
    in_sem, out_sem, og_sem, zs, zr, ss, sr, vs, vr, credit,
):
    width = cot.shape[1]
    blocks = cot.shape[0] // BLK
    tiles = width // BLK
    z = lax.axis_index("tensor")
    d = lax.axis_index("dp")
    loads = [(x_h.at[0, 0], x.at[0, 0]), (wq_h, wq), (wk_h, wk), (wv_h, wv), (x_h.at[0, 1], x.at[0, 1]), (x_h.at[1], x.at[1]),
             (wo_h, wo), (wu_h, wu), (cot_h, cot), (wd_h, wd)]
    loads = [pltpu.make_async_copy(s, t, in_sem.at[i]) for i, (s, t) in enumerate(loads)]
    for c in loads[:4]:
        c.start()
    first = Sums(0, pn, far, tot, zs, zr, FIRST)
    second = Sums(1, pd, n2, tot2, zs, zr, SECOND)
    barrier = pltpu.get_barrier_semaphore()
    if fused:
        for k in range(1, dp):
            pl.semaphore_signal(barrier, inc=1, device_id={"dp": lax.rem(d + k, dp)}, device_id_type=MESH_ID)

    @pl.when(first.end)
    def _():
        pl.semaphore_signal(barrier, inc=1, device_id={"tensor": first.near}, device_id_type=MESH_ID)

    @pl.when(first.middle)
    def _():
        pl.semaphore_signal(barrier, inc=1, device_id={"tensor": first.mate}, device_id_type=MESH_ID)
        pl.semaphore_signal(barrier, inc=1, device_id={"tensor": first.edge}, device_id_type=MESH_ID)

    ends = ends_of(len_ref, n_images)
    m0, m1 = head_masks()
    ones = jnp.ones((BLK, PAIR), BF)
    diagonal = block_diagonal()
    vec[...] = jnp.zeros_like(vec)
    once = jnp.where(z == 1, 1.0, 0.0)
    matrix = lambda ref: ref[...].reshape(width, width)
    apart = pl.when(z >= 0)

    def at_step(j, k, *acts):
        @pl.when(j == k)
        def _():
            for act in acts:
                act()

    def act(kind, which, *more):
        if kind == "add":
            add(which)
        elif kind == "second":
            stage(which)
        elif kind == "last":
            last(which)
        elif kind == "start":
            second.start(which)
        elif kind == "mid":
            (first, second)[which].mid(*more)
        elif which == 0:
            first.tot(*more)
        else:
            second.tot(*more, emit)

    def tick(place, at=None):
        acts = [functools.partial(act, *a) for a in TICKS.get(place, ())]
        if at is None:
            for a in acts:
                a()
        elif acts:
            at_step(*at, *acts)

    def forward_block(b, _):
        rows = pl.ds(pl.multiple_of(b * BLK, BLK), BLK)
        at_step(b, 0, loads[0].wait)
        xb = x[b // 2, lax.rem(b, 2)].reshape(BLK, width).astype(F32)
        hat, _ = normed(xb)
        n1b = (hat * g1[...] + b1[...]).astype(BF)
        n1[:, rows] = n1b.T
        at_step(b, 0, loads[1].wait, loads[6].start, loads[7].start)
        pq[rows, :] = feature(nn(n1b, wq[...]).astype(BF).astype(F32)).astype(BF)
        at_step(b, 0, loads[2].wait, loads[8].start, loads[9].start, loads[4].start, loads[5].start)
        pk[rows, :] = feature(nn(n1b, wk[...]).astype(BF).astype(F32)).astype(BF)
        at_step(b, 0, loads[3].wait)
        va[rows, :] = nn(n1b, wv[...]).astype(BF)
        down, _, cont, trail = block_masks(b, ends)
        down2 = two(down)
        for p in range(width // PAIR):
            lanes = slice(p * PAIR, (p + 1) * PAIR)
            q, k, v = pq[rows, lanes], pk[rows, lanes], va[rows, lanes]
            a = nt(jnp.concatenate([q * m0, q * m1], axis=0), k).astype(BF) * down2
            o = nn(a[:BLK], jnp.concatenate([v * m0, ones * m0], axis=1))
            o = o + nn(a[BLK:], jnp.concatenate([v * m1, ones * m1], axis=1))
            before = jnp.where(b > 0, st[jnp.maximum(b - 1, 0), p].astype(F32), 0.0).astype(BF)
            o = o + nn(q * cont, before)
            st[b, p] = (tn(k * trail, jnp.concatenate([v, ones], axis=1)) * diagonal).astype(BF)
            inverse = 1.0 / o[:, PAIR:]
            rd[rows, lanes] = inverse.astype(BF)
            attended = o[:, :PAIR] * inverse
            attended_low = attended.astype(BF)
            at[rows, lanes] = attended_low
            al[rows, lanes] = (attended - attended_low.astype(F32)).astype(BF)

        @pl.when(b == 0)
        def _():
            count = (dp - 1) if fused else 0
            pl.when(first.end)(lambda: pl.semaphore_wait(barrier, count + 1))
            pl.when(first.middle)(lambda: pl.semaphore_wait(barrier, count + 2))
            for i in range(4, 8):
                loads[i].wait()

        for k in range(1, blocks):
            tick(f"F{k}b", (b, k))
        middle = xb + nn(at[rows, :], wo[...])
        mid[rows, :] = middle
        hat2, _ = normed(middle)
        n2b = (hat2 * g2[...] + b2[...]).astype(BF)
        n2[:, rows] = n2b.T
        at_step(b, 0, loads[8].wait, loads[9].wait)
        cb = cot[rows, :]
        vec[0:1, :] += jnp.sum(cb.astype(F32), axis=0, keepdims=True)
        for c in range(tiles):
            cols = slice(c * BLK, (c + 1) * BLK)
            u = nn(n2b, wu[..., cols].reshape(width, BLK)) + bup[:, cols]
            gh = nt(cb, wd[c].reshape(BLK, width))
            th = jnp.tanh(C0 * (u + C1 * u * u * u))
            hid[rows, cols] = (0.5 * u * (1.0 + th)).astype(BF)
            slope = 0.5 * (1.0 + th) + 0.5 * u * (1.0 - th * th) * (C0 * (1.0 + 3.0 * C1 * u * u))
            gub = (gh * slope).astype(BF)
            gu[rows, cols] = gub
            vec[1:2, cols] += jnp.sum(gub.astype(F32), axis=0, keepdims=True)
        for k in range(1, blocks):
            tick(f"F{k}d", (b, k))
        pn[rows, :] = nt(gu[rows, :], matrix(wu)).astype(BF)
        for k in range(blocks):
            at_step(b, k, *[functools.partial(first.start, c) for c in first.of_block(k)])
        pd[rows, :] = (nn(hid[rows, :], matrix(wd)) + once * (middle + bd[...])).astype(BF)
        for k in range(1, blocks):
            tick(f"F{k}e", (b, k))
        return 0

    lax.fori_loop(0, blocks, forward_block, 0)

    groups = tiles
    jobs = {}
    slots = ((x, rxa), (gwb, rxb), (wu, wd))
    for i, name in enumerate(["up", "down", "out"] + list(range(groups))):
        gw, rx = slots[i % 3]
        jobs[name] = Scatter(i, gw, rx, ss, sr, credit.at[i % 3], 3 * BLK if i > 2 else width)
    last_job = 2 + groups

    def put(name, col, value):
        gw = jobs[name].gw
        gw[..., col:col + value.shape[1]] = value.astype(BF).reshape(gw.shape[:-1] + (value.shape[1],))

    def send_whole(name, targets):
        gw = jobs[name].gw
        copies = []
        for y in range(2):
            for x_ in range(2):
                for k in range(2):
                    row = pl.ds((y * 4 + x_ * 2 + k) * (width // 8), width // 8)
                    for n, (o, col, o_col, wide) in enumerate(targets):
                        copies.append(pltpu.make_async_copy(gw.at[y, x_, k, :, col:col + wide], o.at[row, o_col:o_col + wide],
                                                            og_sem.at[0]))
        for c in copies:
            c.start()
            c.wait()

    def gradient(name, l, r, half):
        wide = width // 2
        for c in range(half * wide, (half + 1) * wide, BLK):
            apart(lambda: put(name, c, nn(l[...], r[:, c:c + BLK])))
        if fused:
            jobs[name].begin(half)
        elif half == 1:
            send_whole(name, [({"up": gu_o, "down": gd_o, "out": go_o}[name], 0, 0, width)])

    def projections(g):
        cols = slice(g * BLK, (g + 1) * BLK)
        apart(lambda: put(g, 0, nn(n1[...], rd[:, cols])))
        apart(lambda: put(g, BLK, nn(n1[...], al[:, cols])))
        if fused:
            jobs[g].begin(0)
        apart(lambda: put(g, 2 * BLK, nn(n1[...], va[:, cols])))
        if fused:
            jobs[g].begin(1)
        else:
            send_whole(g, [(o, i * BLK, g * BLK, BLK) for i, o in enumerate((gq_o, gk_o, gv_o))])

    def turn(ref):
        def part(c, _):
            rows = pl.ds(pl.multiple_of(c * BLK, BLK), BLK)
            gu[:, rows] = ref[rows, :].T
            return 0

        lax.fori_loop(0, blocks, part, 0)

    def ready(name):
        if fused:
            jobs[name].take()
            for c in out_copies({"out": None, 0: "up", 1: "down", 2: "out", 3: 0}[name]) if name != "out" else ():
                c.wait()

    def add(name):
        if fused:
            for h in range(2):
                jobs[name].add(h)

    def stage(name):
        if fused:
            for h in range(2):
                jobs[name].second(h)

    def out_copies(name):
        if name == "down":
            return [pltpu.make_async_copy(ogd, gd_o, og_sem.at[1])]
        s = jobs[name]
        mine = s.gw.at[s.y, s.x, s.core]
        if name in ("up", "out"):
            return [pltpu.make_async_copy(mine, gu_o if name == "up" else go_o, og_sem.at[s.job])]
        return [pltpu.make_async_copy(mine.at[:, i * BLK:(i + 1) * BLK], o.at[:, name * BLK:(name + 1) * BLK],
                                      og_sem.at[3 + 3 * name + i]) for i, o in enumerate((gq_o, gk_o, gv_o))]

    def last(name):
        if not fused:
            return
        s = jobs[name]
        for h in range(2):
            v = s.last(h)
            if name == "down":
                ogd[h * s.half:(h + 1) * s.half, :] = v.T.astype(BF)
            else:
                s.gw[s.y, s.x, s.core, :, s.cols(h)] = v.astype(BF)
        for c in out_copies(name):
            c.start()
        s.sent()
        if s.job + 3 <= last_job:
            s.give()

    if fused:
        jobs["out"].give()
    gradient("up", n2, gu, 0)
    tick("W0")
    gradient("up", n2, gu, 1)
    tick("W1")
    turn(cot)
    gradient("down", gu, hid, 0)
    tick("W2")
    gradient("down", gu, hid, 1)
    tick("W3")

    def reload(b, k):
        return pltpu.make_async_copy(x_h.at[b // 2, lax.rem(b, 2), k],
                                     hid.at[pl.ds(pl.multiple_of(b * BLK + k * PAIR, PAIR), PAIR), :], in_sem.at[2 * b + k])

    for b in range(blocks):
        for k in range(2):
            reload(b, k).start()

    row = lax.broadcasted_iota(jnp.int32, (2 * PAIR, 2 * PAIR), 0) // HEAD
    lane = lax.broadcasted_iota(jnp.int32, (2 * PAIR, 2 * PAIR), 1) // HEAD
    same_head = jnp.where(row == lane, 1.0, 0.0).astype(BF)
    half_lane = lax.rem(lax.broadcasted_iota(jnp.int32, (1, BLK), 1), HEAD) < HEAD // 2

    def norm_block(b):
        rows = pl.ds(pl.multiple_of(b * BLK, BLK), BLK)
        for k in range(blocks):
            if isinstance(b, int):
                for c in first.of_block(k) if k == b else ():
                    first.got(c)
            else:
                at_step(b, k, *[functools.partial(first.got, c) for c in first.of_block(k)])
        hat, scale = normed(mid[rows, :])
        e = tot[rows, :].astype(F32)
        vec[2:3, :] += jnp.sum(e * hat, axis=0, keepdims=True)
        vec[3:4, :] += jnp.sum(e, axis=0, keepdims=True)
        gm = cot[rows, :].astype(F32) + norm_back(e, hat, scale, g2[...])
        mid[rows, :] = gm
        gbb = gm.astype(BF)
        cot[rows, :] = gbb
        ga = nt(gbb, wo[...])
        n = (ga * rd[rows, :].astype(F32)).astype(BF)
        prod = n.astype(F32) * (at[rows, :].astype(F32) + al[rows, :].astype(F32))
        rd[rows, :] = n
        high = prod.astype(BF)
        rest = (prod - high.astype(F32)).astype(BF)
        for c in range(tiles):
            cols = slice(c * BLK, (c + 1) * BLK)
            m = (nn(high[:, cols], same_head) + nn(rest[:, cols], same_head)) * (-2.0 / HEAD)
            m_high = m.astype(BF).astype(F32)
            al[rows, cols] = jnp.where(half_lane, m_high, m - m_high).astype(BF)

    emit = lambda c: pltpu.make_async_copy(tot2.at[second.rows(c), :], out_h.at[second.rows(c), :], out_sem.at[0, c]).start()

    def core_masks(b):
        after_b = jnp.minimum(b + 1, blocks - 1)
        low, up, cont, trail = block_masks(b, ends)
        more = jnp.where(b < blocks - 1, 1.0, 0.0)
        cont_after = (block_masks(after_b, ends)[2].astype(F32) * more).astype(BF)
        return two(low), two(up), cont, trail, cont_after

    def core_pair(b, p, masks):
        low2, up2, cont, trail, cont_after = masks
        rows = pl.ds(pl.multiple_of(b * BLK, BLK), BLK)
        after_rows = pl.ds(pl.multiple_of(jnp.minimum(b + 1, blocks - 1) * BLK, BLK), BLK)
        lanes = slice(p * PAIR, (p + 1) * PAIR)
        q, k, v = pq[rows, lanes], pk[rows, lanes], va[rows, lanes]
        n, m = rd[rows, lanes], al[rows, lanes]
        nm_after = jnp.concatenate([rd[after_rows, lanes], al[after_rows, lanes]], axis=1)
        after = (tn(pq[after_rows, lanes] * cont_after, nm_after) * diagonal).astype(BF)
        q0, q1, k0, k1, n0, n1_ = q * m0, q * m1, k * m0, k * m1, n * m0, n * m1
        nm = jnp.concatenate([n, m], axis=1)
        nm2 = jnp.concatenate(
            [jnp.concatenate([n0, m * m0], axis=1), jnp.concatenate([n1_, m * m1], axis=1)], axis=0
        )
        v1 = jnp.concatenate([v, ones], axis=1)
        v2 = jnp.concatenate(
            [jnp.concatenate([v * m0, ones * m0], axis=1), jnp.concatenate([v * m1, ones * m1], axis=1)], axis=0
        )
        da = nt(nm2, v1).astype(BF) * low2
        dat = nt(v2, nm).astype(BF) * up2
        a_t = nt(jnp.concatenate([k0, k1], axis=0), q).astype(BF) * up2
        before = jnp.where(b > 0, st[jnp.maximum(b - 1, 0), p].astype(F32), 0.0).astype(BF)
        dq = nn(da[:BLK], k0) + nn(da[BLK:], k1) + nt(nm * cont, before)
        dk = nn(dat[:BLK], q0) + nn(dat[BLK:], q1) + nt(v1 * trail, after)
        dv = nn(a_t[:BLK], n0) + nn(a_t[BLK:], n1_) + nn(k * trail, after[:, :PAIR])
        rd[rows, lanes] = (dq * jnp.minimum(q.astype(F32), 1.0)).astype(BF)
        al[rows, lanes] = (dk * jnp.minimum(k.astype(F32), 1.0)).astype(BF)
        va[rows, lanes] = dv.astype(BF)

    def input_block(b):
        rows = pl.ds(pl.multiple_of(b * BLK, BLK), BLK)
        e = nt(rd[rows, :], wq[...]) + nt(al[rows, :], wk[...]) + nt(va[rows, :], wv[...])
        for k in range(2):
            reload(b, k).wait()
        hat, scale = normed(hid[rows, :].astype(F32))
        vec[4:5, :] += jnp.sum(e * hat, axis=0, keepdims=True)
        vec[5:6, :] += jnp.sum(e, axis=0, keepdims=True)
        hid[rows, :] = (mid[rows, :] + norm_back(e, hat, scale, g1[...])).astype(BF)
        pltpu.make_async_copy(hid.at[rows, :], gi_h.at[rows, :], out_sem.at[1, b]).start()

    def backward_step(j, _):
        for k in range(blocks - 1):
            tick(f"J{k}n", (j, k))
        apart(lambda: norm_block(j))
        for k in range(blocks - 1):
            tick(f"J{k}a", (j, k))

        @pl.when(j > 0)
        def _():
            masks = core_masks(j - 1)
            for p in range(width // PAIR):
                core_pair(j - 1, p, masks)
                for k in range(1, blocks - 1):
                    tick(f"J{k}p{p}", (j, k))
            apart(lambda: input_block(j - 1))

        for k in range(1, blocks - 1):
            tick(f"J{k}e", (j, k))
        return 0

    lax.fori_loop(0, blocks - 1, backward_step, 0)
    apart(lambda: norm_block(blocks - 1))
    tick("N3")
    ready("out")
    turn(at)
    gradient("out", gu, cot, 0)
    tick("O0")
    gradient("out", gu, cot, 1)
    tick("O1")

    def late_group(b, g):
        masks = core_masks(b)
        for p in (2 * g, 2 * g + 1):
            core_pair(b, p, masks)

    for g in range(groups):
        apart(functools.partial(late_group, blocks - 2, g))
        tick(f"G{g}a")
        apart(functools.partial(late_group, blocks - 1, g))
        tick(f"G{g}b")
        ready(g)
        projections(g)
        tick(f"G{g}c")
    apart(lambda: input_block(blocks - 2))
    tick("I2")
    apart(lambda: input_block(blocks - 1))
    tick("I3")
    if fused:
        own = pl.ds(pl.multiple_of(d * (width // dp), width // dp), width // dp)
        small = []
        for k in range(1, dp):
            to = lax.rem(d + k, dp)
            cols = pl.ds(pl.multiple_of(to * (width // dp), width // dp), width // dp)
            small.append(pltpu.make_async_remote_copy(
                src_ref=vec.at[:, cols], dst_ref=rv.at[k], send_sem=vs.at[k], recv_sem=vr.at[k],
                device_id={"dp": to}, device_id_type=MESH_ID))
        for c in small:
            c.start()
    tick("END")
    if fused:
        total = vec[:, own]
        for c in small:
            c.wait_recv()
        for k in range(1, dp):
            total = total + rv[k]
        vec_o[...] = total
        for c in small:
            c.wait_send()
    else:
        vec_o[...] = vec[...]
    for c in range(len(SECOND)):
        second.got(c, emit)
    for c in range(len(FIRST)):
        first.finish(c)
    for c in range(len(SECOND)):
        second.finish(c)
        pltpu.make_async_copy(tot2.at[second.rows(c), :], out_h.at[second.rows(c), :], out_sem.at[0, c]).wait()
    for b in range(blocks):
        rows = pl.ds(b * BLK, BLK)
        pltpu.make_async_copy(hid.at[rows, :], gi_h.at[rows, :], out_sem.at[1, b]).wait()
    if fused:
        for name in (1, 2, 3):
            for c in out_copies(name):
                c.wait()


def finish_kernel(out_h, gi_h, *refs):
    weights, vec = refs[:6], refs[6]
    out_o, gi_o = refs[7:9]
    weights_o, vecs_o = refs[9:15], refs[15:21]
    narrow, wide, small, small_wide, tall, tall_wide, passed, sem_in, sem_out, sem = refs[21:]
    rows = gi_h.shape[0] // 8
    part = lambda c: pl.ds(c * rows, rows)
    ins = [pltpu.make_async_copy(gi_h.at[part(c), :], narrow.at[part(c), :], sem_in.at[c]) for c in range(8)]
    outs = [pltpu.make_async_copy(wide.at[part(c), :], gi_o.at[part(c), :], sem_out.at[c]) for c in range(8)]
    where = [(tall, tall_wide) if i == 1 else (small.at[i], small_wide.at[i]) for i in range(6)]
    ins += [pltpu.make_async_copy(weights[i], where[i][0], sem_in.at[8 + i]) for i in range(6)]
    outs += [pltpu.make_async_copy(where[i][1], weights_o[i], sem_out.at[8 + i]) for i in range(6)]
    through = [[pltpu.make_async_copy(s.at[part(c), :], t.at[part(c), :], sem.at[i, c])
                for i, (s, t) in enumerate(((out_h, passed), (passed, out_o)))] for c in range(8)]
    for c in range(8):
        through[c][0].start()
        ins[c].start()
    for c in ins[8:]:
        c.start()
    for i, o in enumerate(vecs_o):
        o[...] = vec[i, :]
    for c in range(8):
        through[c][0].wait()
        through[c][1].start()
        ins[c].wait()
        wide[part(c), :] = narrow[part(c), :].astype(F32)
        outs[c].start()
    for i in range(6):
        ins[8 + i].wait()
        where[i][1][...] = where[i][0][...].astype(F32)
        outs[8 + i].start()
    for c in outs:
        c.wait()
    for c in through:
        c[1].wait()


def per_device(dp, inputs, cotangent, lengths, ln1_gain, ln1_bias, w_query, w_key, w_value, w_out, ln2_gain, ln2_bias, w_up, b_up,
               w_down, b_down):
    tokens, width = inputs.shape
    n_images = lengths.shape[1]
    fused = dp == 8
    blocks, pairs = tokens // BLK, width // PAIR
    shape = jax.ShapeDtypeStruct
    full = shape((tokens, width), BF)
    piece, square = shape((width // dp, width), BF), shape((width, width), BF)
    tall = shape((width, width // dp), BF)
    anyspace = pl.BlockSpec(memory_space=pl.ANY)
    vmem = pl.BlockSpec(memory_space=VM)
    smem = pl.BlockSpec(memory_space=pltpu.SMEM)
    row = lambda v: v.reshape(1, -1)
    big = lambda dtype=BF: VM((tokens, width), dtype)
    weight = VM((width, width), BF)
    split = (2, 2, 2, width // 8, width)
    boxed = VM(split, BF)
    received = VM((4, 2, width // 8, width), BF)
    dma = pltpu.SemaphoreType.DMA
    weights_out = [piece, tall] + [piece] * 4 if fused else [square] * 6
    pieces = max(len(FIRST), len(SECOND))
    outs = pl.pallas_call(
        functools.partial(layer_kernel, n_images, fused, dp),
        out_shape=[full, full] + weights_out + [shape((8, width // dp if fused else width), F32)],
        in_specs=[smem] + [vmem] * 6 + [anyspace] * 8,
        out_specs=[anyspace] * 8 + [vmem],
        scratch_shapes=[boxed, big()] + [weight] * 4 + [boxed, received] + [big()] * 7
        + [VM((blocks, pairs, PAIR, 2 * PAIR), BF), big(F32)] + [big()] * 8
        + [boxed, received, received, VM((width, width // 8), BF), VM((8, width), F32),
           VM((8, 8, width // 8), F32)]
        + [dma((10,)), dma((2, pieces)), dma((15,)), dma((2, 2, pieces)), dma((2, 2, pieces)), dma((7, 3, 2)), dma((7, 3, 2)),
           dma((8,)), dma((8,)), pltpu.SemaphoreType.REGULAR((3,))],
        compiler_params=pltpu.CompilerParams(vmem_limit_bytes=VMEM_LIMIT, collective_id=0, has_side_effects=True),
    )(lengths, row(ln1_gain), row(ln1_bias), row(ln2_gain), row(ln2_bias), row(b_up), row(b_down),
      inputs.reshape(split), cotangent, w_query, w_key, w_value, w_out, w_up.reshape(split), w_down.reshape(4, 2, width // 8, width))
    out, gi, gu, gd, go, gq, gk, gv, vec = outs
    if fused:
        wide = lambda s: shape(s.shape, F32)
        small = shape((width // dp,), F32)
        outs = pl.pallas_call(
            finish_kernel,
            out_shape=[full, wide(full)] + [wide(s) for s in weights_out] + [small] * 6,
            in_specs=[anyspace] * 8 + [vmem],
            out_specs=[anyspace] * 8 + [vmem] * 6,
            scratch_shapes=[big(), big(F32), VM((6,) + piece.shape, BF), VM((6,) + piece.shape, F32), VM(tall.shape, BF),
                            VM(tall.shape, F32), big(), dma((14,)), dma((14,)), dma((2, 8))],
            compiler_params=pltpu.CompilerParams(vmem_limit_bytes=VMEM_LIMIT),
        )(out, gi, gu, gd, go, gq, gk, gv, vec)
        out, gi, gu, gd, go, gq, gk, gv = outs[:8]
        vec = outs[8:]
    else:
        scatter = lambda v, axis=0: lax.psum_scatter(v, "dp", scatter_dimension=axis, tiled=True)
        gu, go, gq, gk, gv = (scatter(v).astype(F32) for v in (gu, go, gq, gk, gv))
        gd = scatter(gd).astype(F32).T
        vec = scatter(vec, 1)
        gi = gi.astype(F32)
    return (out, gi, vec[4], vec[5], gq, gk, gv, go, vec[2], vec[3], gu, vec[1], gd, vec[0])


VMEM_LIMIT = 64 << 20


def solution(mesh):
    rows, whole = P("dp", None), P()
    placed = (rows, rows, rows) + (whole,) * 8 + (P(None, "tensor"), P("tensor"), P("tensor", None), whole)
    return jax.shard_map(
        functools.partial(per_device, mesh.shape["dp"]),
        mesh=mesh,
        in_specs=placed,
        out_specs=(rows, rows, P("dp"), P("dp"), rows, rows, rows, rows, P("dp"), P("dp"), P("dp", "tensor"),
                   P(("tensor", "dp")), P("tensor", "dp"), P("dp")),
        check_vma=False,
    )
```
